128 devices in a mesh: ep: 32 (over x, z, core), edp: 4 (over y).
Axes of the slice: x: 4, y: 4, z: 4, core: 2. Of those that a mesh axis runs over, the one named last changes fastest.
Arguments:
- tokens: bfloat16 [24576, 3584], P(('ep', 'edp')), may hold values from -6 to 6
- upstream: bfloat16 [24576, 3584], P(('ep', 'edp')), may hold values from -3 to 3
- expert_ids: int32 [24576, 2], P(('ep', 'edp')), may hold values from 0 to 31, all different within a row; in each aligned block of 192 rows (0 to 191, 192 to 383, ...) at most 15 rows name the same one
- gate_values: bfloat16 [24576, 2], P(('ep', 'edp')), may hold values from 0.049804688 to 0.59765625
- w_gate: bfloat16 [32, 3584, 1024], P('ep', 'edp'), may hold values from -0.09375 to 0.09375
- w_up: bfloat16 [32, 3584, 1024], P('ep', 'edp'), may hold values from -0.09375 to 0.09375
- w_down: bfloat16 [32, 3584, 1024], P('ep', 'edp'), may hold values from -0.1875 to 0.1875
Outputs:
- token_grad: bfloat16 [24576, 3584], P(('ep', 'edp'))
- gate_grad: bfloat16 [24576, 2], P(('ep', 'edp'))
- grad_gate: bfloat16 [32, 3584, 1024], P('ep', 'edp')
- grad_up: bfloat16 [32, 3584, 1024], P('ep', 'edp')
- grad_down: bfloat16 [32, 3584, 1024], P('ep', 'edp')
The draws below stay inside these ranges and needn't reach their ends.
Inputs may be any that keep to these rules, and one draw needn't show every extreme that they name: `expert_ids`: the 2 ids of a token differ. Among the rows of one device (aligned blocks of 192 tokens) no expert is named more than 15 times, and in every draw some device names some expert exactly 15 times.
All inputs are finite; a program needn't handle non-finite values.
Results may differ from the reference program's by a relative error of at most 0.013.
Values may be sent and summed in bfloat16 or wider, within the bound.
A program may use at most 192 MiB of HBM per device.

```python
import math
import jax
import jax.numpy as jnp
import numpy as np
from jax import lax

D = 3584
FF = 1024
TOP = 2
TOK_DEV = 192
EXPERTS = 32
CAP = 15
TOKENS = 24576
N_EP = 32
N_EDP = 4


def steps_of(key, extent, cuts, low, largest):
    level, own = 1.0, jax.random.fold_in(key, 6)
    for position, shards_of in cuts:
        heights = jnp.exp(jax.random.uniform(jax.random.fold_in(own, position), (shards_of,), jnp.float32, low / len(cuts), largest / len(cuts)))
        level = level * jnp.repeat(heights, extent[position] // shards_of).reshape([-1 if axis == position else 1 for axis in range(len(extent))])
    return level


def routed_block(own_key, own, number, rows, amount, top, reach, slope):
    sequence = jax.random.permutation(own_key, amount)
    heavy_load, common = portions_of(amount, rows * top, reach, slope, True), portions_of(amount, rows * top, reach, slope, False)
    places = jnp.arange(amount)

    def named(sizes, turn):
        used = int((sizes > 0).sum())
        fixed = max(1, used // 4)
        moved = fixed + (places - fixed + turn * (used - fixed)) % max(1, amount - fixed)
        return jnp.zeros((amount,), jnp.int32).at[sequence[jnp.where(places < fixed, places, moved)]].set(jnp.asarray(sizes, jnp.int32))

    sizes = jnp.where(number % 4 == 0, named(heavy_load, number // 4), named(common, number - number // 4 - 1))
    mixed = jax.random.permutation(jax.random.fold_in(own, 3), amount)
    donor, sink = mixed[0:amount // 2 * 2:2], mixed[1:amount // 2 * 2:2]
    room = jnp.minimum(sizes[donor] - 1, reach - sizes[sink]) // 2
    room = jnp.where((donor == sequence[0]) | (sink == sequence[0]) | (sizes[sink] == 0), 0, jnp.maximum(room, 0))
    moved = jax.random.randint(jax.random.fold_in(own, 4), (amount // 2,), 0, 1 << 20) % (room + 1)
    sizes = sizes.at[donor].add(-moved).at[sink].add(moved)
    items = jnp.searchsorted(jnp.cumsum(sizes), jnp.arange(rows * top), side="right").astype(jnp.int32)
    grid = items.reshape(top, rows).T
    grid = grid[jax.random.permutation(jax.random.fold_in(own, 1), rows)]
    turn = jax.random.randint(jax.random.fold_in(own, 2), (rows, 1), 0, top)
    return jnp.take_along_axis(grid, (jnp.arange(top)[None, :] + turn) % top, axis=1)


def portions_of(count, total, limit, skew, full):
    loads = [(1 << 20) // math.isqrt(rank ** skew) + 1 for rank in range(1, count + 1)]
    largest = limit if full else min(limit, max(-(-total // count), total * loads[0] // sum(loads)))
    least = 1 if total - largest >= count - 1 else 0
    given, spare = [largest] + [least] * (count - 1), total - largest - least * (count - 1)
    while spare > 0:
        candidates = [i for i in range(1, count) if given[i] < largest] or [i for i in range(1, count) if given[i] < limit]
        whole, budget = sum([loads[i] for i in candidates]), spare
        for i in candidates:
            extra = min(limit - given[i], max(1, budget * loads[i] // whole), spare)
            given[i] = given[i] + extra
            spare = spare - extra
    return np.array(given)


def scatter_about(own_key, extent, scale, bound, pieces=(), held_as=jnp.bfloat16):
    factor_of = steps_of(own_key, extent, pieces, -0.22, 0.18) if pieces else 1.0
    values = jax.random.normal(own_key, extent, jnp.float32) * scale * factor_of
    return jnp.minimum(jnp.maximum(values, -bound), bound).astype(held_as)


def setup_inputs(seed: int = 0) -> dict:
    streams_of = jax.random.split(jax.random.key(seed), 8)
    tokens = scatter_about(streams_of[0], (TOKENS, D), 1.0, 6.0, ((0, 128),))
    upstream = scatter_about(streams_of[1], (TOKENS, D), 0.5, 3.0, ((0, 128),))
    expert_ids_keys = jax.random.split(jax.random.fold_in(streams_of[2], 1), TOKENS // TOK_DEV)
    expert_ids_turns = jax.random.permutation(jax.random.fold_in(streams_of[2], 3), TOKENS // TOK_DEV)
    expert_ids = jax.vmap(lambda own, number: routed_block(jax.random.fold_in(streams_of[2], 2), own, number, TOK_DEV, EXPERTS, TOP, CAP, 2))(expert_ids_keys, expert_ids_turns).reshape((TOKENS, TOP))
    gate_values = jnp.clip(0.049804688 + 0.54785156 * jax.random.uniform(streams_of[3], (TOKENS, TOP), jnp.float32) ** steps_of(streams_of[3], (TOKENS, TOP), ((0, 128),), -0.2, 0.2), 0.049804688, 0.59765625).astype(jnp.bfloat16)
    w_gate = scatter_about(streams_of[4], (EXPERTS, D, FF), D ** -0.5, 0.09375, ((0, 32), (1, 4)))
    w_up = scatter_about(streams_of[5], (EXPERTS, D, FF), D ** -0.5, 0.09375, ((0, 32), (1, 4)))
    w_down = scatter_about(streams_of[6], (EXPERTS, D, FF), FF ** -0.5, 0.1875, ((0, 32), (1, 4)))
    return dict(tokens=tokens, upstream=upstream, expert_ids=expert_ids, gate_values=gate_values, w_gate=w_gate, w_up=w_up, w_down=w_down)


def expert_backward(x_rows, dy_rows, gate_rows, gate_w, up_w, down_w):
    pre_gate = jnp.dot(x_rows, gate_w, preferred_element_type=jnp.float32)
    pre_up = jnp.dot(x_rows, up_w, preferred_element_type=jnp.float32)
    back = jnp.dot(dy_rows, down_w, preferred_element_type=jnp.float32)
    sigma = jax.nn.sigmoid(pre_gate)
    silu_val = pre_gate * sigma
    act = (silu_val * pre_up).astype(jnp.bfloat16)
    act_f = act.astype(jnp.float32)
    gate_out = jnp.sum(act_f * back, axis=1).astype(jnp.bfloat16)
    weight_f = gate_rows.astype(jnp.float32)[:, None]
    d_act = weight_f * back
    d_gate_pre = (d_act * pre_up * sigma * (1.0 + pre_gate * (1.0 - sigma))).astype(jnp.bfloat16)
    d_up_pre = (d_act * silu_val).astype(jnp.bfloat16)
    scaled_act = (weight_f * act_f).astype(jnp.bfloat16)
    contract = (((1,), (1,)), ((), ()))
    reply = lax.dot_general(d_gate_pre, gate_w, contract, preferred_element_type=jnp.float32)
    reply = reply + lax.dot_general(d_up_pre, up_w, contract, preferred_element_type=jnp.float32)
    return reply.astype(jnp.bfloat16), gate_out, d_gate_pre, d_up_pre, scaled_act


def reference(tokens, upstream, expert_ids, gate_values, w_gate, w_up, w_down):
    devices = N_EP * N_EDP
    per_dev = TOK_DEV * TOP
    route_ids = expert_ids.reshape(devices, per_dev).astype(jnp.int32)
    onehot = (route_ids[:, :, None] == jnp.arange(EXPERTS, dtype=jnp.int32)[None, None, :]).astype(jnp.int32)
    slot_idx = jnp.sum(jnp.cumsum(onehot, axis=1) * onehot, axis=2) - 1
    dev_idx = jnp.broadcast_to(jnp.arange(devices, dtype=jnp.int32)[:, None], route_ids.shape)
    pair_idx = jnp.broadcast_to(jnp.arange(per_dev, dtype=jnp.int32)[None, :], route_ids.shape)
    slot_table = jnp.full((devices, EXPERTS, CAP), -1, jnp.int32).at[dev_idx, route_ids, slot_idx].set(pair_idx)
    flat_gates = gate_values.reshape(-1)

    def expert_step(carry, inputs):
        grad_acc, gate_acc = carry
        expert_idx, gate_w, up_w, down_w = inputs
        totals = jnp.zeros((D, 3 * FF), jnp.float32)
        for group_id in range(N_EDP):
            sources = jnp.arange(N_EP, dtype=jnp.int32) * N_EDP + group_id
            entries = slot_table[sources, expert_idx].reshape(-1)
            is_valid = entries >= 0
            safe_idx = jnp.where(is_valid, entries, 0).astype(jnp.int32)
            source_row = jnp.repeat(sources, CAP).astype(jnp.int32)
            token_row = (source_row * TOK_DEV + safe_idx // TOP).astype(jnp.int32)
            assign_row = (source_row * per_dev + safe_idx).astype(jnp.int32)
            zero_b = jnp.zeros((), jnp.bfloat16)
            x_rows = jnp.where(is_valid[:, None], tokens[token_row], zero_b)
            dy_rows = jnp.where(is_valid[:, None], upstream[token_row], zero_b)
            gate_rows = jnp.where(is_valid, flat_gates[assign_row], zero_b)
            reply, gate_out, d_gate_pre, d_up_pre, scaled_act = expert_backward(x_rows, dy_rows, gate_rows, gate_w, up_w, down_w)
            grad_acc = grad_acc.at[token_row].add(jnp.where(is_valid[:, None], reply.astype(jnp.float32), jnp.zeros((), jnp.float32)))
            gate_acc = gate_acc.at[assign_row].add(jnp.where(is_valid, gate_out.astype(jnp.float32), jnp.zeros((), jnp.float32)))
            partial_value = jnp.concatenate([
                jnp.dot(x_rows.T, d_gate_pre, preferred_element_type=jnp.float32),
                jnp.dot(x_rows.T, d_up_pre, preferred_element_type=jnp.float32),
                jnp.dot(dy_rows.T, scaled_act, preferred_element_type=jnp.float32)], axis=1)
            totals = totals + lax.optimization_barrier(partial_value.astype(jnp.bfloat16)).astype(jnp.float32)
        stacked = totals.astype(jnp.bfloat16)
        return (grad_acc, gate_acc), (stacked[:, :FF], stacked[:, FF:2 * FF], stacked[:, 2 * FF:])

    init = (jnp.zeros((TOKENS, D), jnp.float32), jnp.zeros((TOKENS * TOP,), jnp.float32))
    (grad_acc, gate_acc), grads = lax.scan(expert_step, init, (jnp.arange(EXPERTS, dtype=jnp.int32), w_gate, w_up, w_down))
    token_grad = grad_acc.astype(jnp.bfloat16)
    gate_grad = gate_acc.reshape(TOKENS, TOP).astype(jnp.bfloat16)
    return token_grad, gate_grad, grads[0], grads[1], grads[2]
```

```python
import functools

import jax
import jax.numpy as jnp
from jax import lax
from jax.experimental import pallas as pl
from jax.experimental.pallas import tpu as pltpu
from jax.sharding import PartitionSpec as P

MESH = pl.DeviceIdType.MESH
ROWS = 16


def place():
    ep, plane = lax.axis_index("ep"), lax.axis_index("edp")
    core = lax.rem(ep, 2)
    parity = plane // 2
    beside = plane + 1 - 2 * lax.rem(plane, 2)
    across = 3 - plane
    return ep, ep // 2, core, plane, parity, beside, across


def remote(src, dst, send, recv, ep, plane):
    return pltpu.make_async_remote_copy(
        src_ref=src, dst_ref=dst, send_sem=send, recv_sem=recv,
        device_id=(ep, plane), device_id_type=MESH,
    )


def landed(ref, sem):
    pltpu.make_async_copy(ref, ref, sem).wait()


def gather_kernel(chips, x_send, dy_send, w_gate, w_up, w_down, x_all, dy_all, f_gate, f_up, f_down,
                  local_sem, token_send, token_recv, pass_send, pass_recv,
                  weight_send, weight_recv, relay_send):
    ep, chip, core, plane, parity, beside, across = place()
    depth, width = w_gate.shape
    half = width // 2
    sibling = ep + 1 - 2 * core
    shards = (w_gate, w_up, w_down)
    fulls = (f_gate, f_up, f_down)

    def rows_of(ref, shard):
        return ref.at[pl.ds(pl.multiple_of(shard * depth, 16), depth)]

    def columns(ref, part):
        return ref.at[:, pl.ds(pl.multiple_of(part * half, 128), half)]

    away = core != parity
    for m in range(3):
        @pl.when(away)
        def _(m=m):
            for part in range(2):
                remote(columns(shards[m], part), rows_of(fulls[m], plane), weight_send.at[m, part],
                       weight_recv.at[m, 0], 2 * chip + part, across).start()

    for n, (source, target) in enumerate(((x_send, x_all), (dy_send, dy_all))):
        for group in range(2):
            def send(k, carry, n=n, group=group, source=source, target=target):
                to = lax.rem(chip + k, chips)
                to_plane = plane if group == 0 else across
                kind = parity if group == 0 else 1 - parity
                remote(source.at[2 * to + kind], target.at[core, group, chip], token_send.at[n, group],
                       token_recv.at[n, group], 2 * to + core, to_plane).start()
                return carry

            if group == 0:
                pltpu.make_async_copy(source.at[2 * chip + parity], target.at[core, 0, chip],
                                      token_recv.at[n, 0]).start()
            lax.fori_loop(1 if group == 0 else 0, chips, send, 0)
        if n == 0:
            for m in range(3):
                @pl.when(jnp.logical_not(away))
                def _(m=m):
                    for part in range(2):
                        remote(columns(shards[m], part), rows_of(fulls[m], plane), weight_send.at[m, part],
                               weight_recv.at[m, 1], 2 * chip + part, beside).start()
                    pltpu.make_async_copy(columns(shards[m], core), rows_of(fulls[m], plane),
                                          weight_recv.at[m, 2]).start()
                    remote(columns(shards[m], 1 - core), rows_of(fulls[m], plane), weight_send.at[m, 2],
                           weight_recv.at[m, 2], sibling, plane).start()

    def relay(m):
        return remote(rows_of(fulls[m], across), rows_of(fulls[m], across), relay_send.at[m],
                      weight_recv.at[m, 3], 2 * chip + core, beside)

    def hand_over(n, group):
        target = (x_all, dy_all)[n]
        return remote(target.at[core, group], target.at[core, group], pass_send.at[n, group],
                      pass_recv.at[n, group], sibling, plane)

    for m in range(2):
        landed(rows_of(fulls[m], across), weight_recv.at[m, 0])
        relay(m).start()
    for group in range(2):
        landed(x_all.at[core, group], token_recv.at[0, group])
        hand_over(0, group).start()
    landed(rows_of(fulls[2], across), weight_recv.at[2, 0])
    relay(2).start()
    for group in range(2):
        landed(dy_all.at[core, group], token_recv.at[1, group])
        hand_over(1, group).start()

    for m in range(3):
        landed(rows_of(fulls[m], beside), weight_recv.at[m, 1])
        landed(rows_of(fulls[m], plane), weight_recv.at[m, 2])
        landed(rows_of(fulls[m], 3 - beside), weight_recv.at[m, 3])
        relay(m).wait_send()
        for part in range(2):
            landed(columns(shards[m], part), weight_send.at[m, part])

        @pl.when(jnp.logical_not(away))
        def _(m=m):
            landed(columns(shards[m], 0), weight_send.at[m, 2])
    for n, target in enumerate((x_all, dy_all)):
        for group in range(2):
            hand_over(n, group).wait_send()
            landed(target.at[1 - core, group], pass_recv.at[n, group])
        landed(target.at[core, 0, pl.ds(0, chips - 1)], token_send.at[n, 0])
        landed(target.at[core, 1], token_send.at[n, 1])


def return_kernel(chips, reply, gates, t_gate, t_up, t_down, reply_out, gates_out, g_gate, g_up, g_down,
                  reply_own, reply_in, gates_own, gates_in, sums, arrived,
                  local_sem, pass_send, pass_recv, sum_send, sum_recv, out_send, out_recv,
                  back_send, back_recv):
    ep, chip, core, plane, parity, beside, across = place()
    width = g_gate.shape[1]
    half = width // 2
    sibling = ep + 1 - 2 * core
    terms = (t_gate, t_up, t_down)
    outs = (g_gate, g_up, g_down)

    def columns(ref, part):
        return ref.at[:, pl.ds(pl.multiple_of(part * half, 128), half)]

    passes = [
        remote(reply.at[1 - core], reply_in, pass_send.at[0], pass_recv.at[0], sibling, plane),
        remote(gates.at[1 - core], gates_in, pass_send.at[1], pass_recv.at[1], sibling, plane),
    ]
    loads = [
        pltpu.make_async_copy(reply.at[core], reply_own, local_sem.at[0]),
        pltpu.make_async_copy(gates.at[core], gates_own, local_sem.at[1]),
    ]
    for copy in passes + loads:
        copy.start()
    moves = {}
    for s in (1, 0):
        for m in range(3):
            theirs = 3 - beside if s else beside
            mine = across if s else plane
            moves[m, s] = (
                remote(terms[m].at[theirs], arrived.at[m, s], sum_send.at[m, s], sum_recv.at[m, s],
                       2 * chip + core, beside),
                pltpu.make_async_copy(terms[m].at[mine], sums.at[m, s], local_sem.at[2 + 2 * m + s]),
            )
            for copy in moves[m, s]:
                copy.start()

    for copy in loads:
        copy.wait()
    for copy in passes:
        copy.wait()

    def add_reply(k, carry):
        group, row = k // chips, lax.rem(k, chips)
        total = reply_own[group, row].astype(jnp.float32) + reply_in[group, row].astype(jnp.float32)
        reply_own[group, row] = total.astype(reply_own.dtype)
        gates_own[group, row] = gates_own[group, row] + gates_in[group, row]
        return carry

    lax.fori_loop(0, 2 * chips, add_reply, 0)
    for group in range(2):
        def send(k, carry, group=group):
            to = lax.rem(chip + k, chips)
            to_plane = plane if group == 0 else across
            remote(reply_own.at[group, to], reply_out.at[2 * chip + parity], back_send.at[0, group],
                   back_recv.at[0, group], 2 * to + core, to_plane).start()
            remote(gates_own.at[group, to], gates_out.at[2 * chip + parity], back_send.at[1, group],
                   back_recv.at[1, group], 2 * to + core, to_plane).start()
            return carry

        if group == 0:
            pltpu.make_async_copy(reply_own.at[0, chip], reply_out.at[2 * chip + parity],
                                  back_recv.at[0, 0]).start()
            pltpu.make_async_copy(gates_own.at[0, chip], gates_out.at[2 * chip + parity],
                                  back_recv.at[1, 0]).start()
        lax.fori_loop(1 if group == 0 else 0, chips, send, 0)

    for s in (1, 0):
        for m in range(3):
            for copy in moves[m, s]:
                copy.wait()
            step = 128

            def add(k, carry, m=m, s=s):
                rows = pl.ds(pl.multiple_of(k * step, step), step)
                total = sums[m, s, rows].astype(jnp.float32) + arrived[m, s, rows].astype(jnp.float32)
                sums[m, s, rows] = total.astype(sums.dtype)
                return carry

            lax.fori_loop(0, sums.shape[2] // step, add, 0)
            if s:
                remote(sums.at[m, 1], columns(outs[m], core), out_send.at[m, 1], out_recv.at[m, core],
                       2 * chip + parity, across).start()
            else:
                @pl.when(core == parity)
                def _(m=m):
                    pltpu.make_async_copy(sums.at[m, 0], columns(outs[m], core), out_recv.at[m, core]).start()

                @pl.when(core != parity)
                def _(m=m):
                    remote(sums.at[m, 0], columns(outs[m], core), out_send.at[m, 0], out_recv.at[m, core],
                           2 * chip + parity, plane).start()

    for m in range(3):
        landed(sums.at[m, 1], out_send.at[m, 1])

        @pl.when(core != parity)
        def _(m=m):
            landed(sums.at[m, 0], out_send.at[m, 0])
        for part in range(2):
            landed(columns(outs[m], part), out_recv.at[m, part])
    for n, (own, out) in enumerate(((reply_own, reply_out), (gates_own, gates_out))):
        landed(own.at[0, pl.ds(0, chips - 1)], back_send.at[n, 0])
        landed(own.at[1], back_send.at[n, 1])
        for group in range(2):
            landed(own.at[group], back_recv.at[n, group])


def expert_backward(x_rows, dy_rows, gate_w, up_w, down_w):
    pre_gate = jnp.dot(x_rows, gate_w, preferred_element_type=jnp.float32)
    pre_up = jnp.dot(x_rows, up_w, preferred_element_type=jnp.float32)
    back = jnp.dot(dy_rows, down_w, preferred_element_type=jnp.float32)
    sigma = jax.nn.sigmoid(pre_gate)
    silu_val = pre_gate * sigma
    act = (silu_val * pre_up).astype(jnp.bfloat16)
    gate_out = jnp.sum(act.astype(jnp.float32) * back, axis=1, keepdims=True)
    d_gate_pre = (back * pre_up * sigma * (1.0 + pre_gate * (1.0 - sigma))).astype(jnp.bfloat16)
    d_up_pre = (back * silu_val).astype(jnp.bfloat16)
    contract = (((1,), (1,)), ((), ()))
    reply = lax.dot_general(d_gate_pre, gate_w, contract, preferred_element_type=jnp.float32)
    reply = reply + lax.dot_general(d_up_pre, up_w, contract, preferred_element_type=jnp.float32)
    return reply.astype(jnp.bfloat16), gate_out, d_gate_pre, d_up_pre, act


def over_rows(left, right):
    return lax.dot_general(left, right, (((0,), (0,)), ((), ())), preferred_element_type=jnp.float32)


def shards(tokens, upstream, expert_ids, gate_values, w_gate, w_up, w_down):
    experts = lax.axis_size("ep")
    chips = experts // 2
    tok_count, top_count = expert_ids.shape
    model_width = tokens.shape[1]
    depth, width = w_gate.shape[1:]
    half = width // 2
    buffer_rows = experts * ROWS
    bf16 = jnp.bfloat16
    flat_ids = expert_ids.reshape(-1)
    onehot = (flat_ids[:, None] == jnp.arange(experts, dtype=jnp.int32)[None, :]).astype(jnp.int32)
    slot_idx = jnp.sum(jnp.cumsum(onehot, axis=0) * onehot, axis=1) - 1
    target = (flat_ids * ROWS + slot_idx).reshape(tok_count, top_count)
    slots = jnp.arange(buffer_rows, dtype=jnp.int32)
    picks = [slots[:, None] == target[None, :, k] for k in range(top_count)]
    zero = jnp.zeros((), bf16)
    dispatch_map = sum(pick.astype(bf16) for pick in picks)
    scaled_map = sum(jnp.where(pick, gate_values[None, :, k], zero) for k, pick in enumerate(picks))
    x_send = jnp.dot(dispatch_map, tokens, preferred_element_type=jnp.float32).astype(bf16)
    dy_send = jnp.dot(scaled_map, upstream, preferred_element_type=jnp.float32).astype(bf16)

    anywhere = pl.BlockSpec(memory_space=pl.ANY)
    dma = pltpu.SemaphoreType.DMA
    rows_shape = jax.ShapeDtypeStruct((2, 2, chips, ROWS, model_width), bf16)
    full_shape = jax.ShapeDtypeStruct((4 * depth, half), bf16)
    x_all, dy_all, f_gate, f_up, f_down = pl.pallas_call(
        functools.partial(gather_kernel, chips),
        out_shape=[rows_shape] * 2 + [full_shape] * 3,
        in_specs=[anywhere] * 5,
        out_specs=[anywhere] * 5,
        scratch_shapes=[dma((2,)), dma((2, 2)), dma((2, 2)), dma((2, 2)), dma((2, 2)),
                        dma((3, 3)), dma((3, 4)), dma((3,))],
        compiler_params=pltpu.CompilerParams(has_side_effects=True),
        name="gather_rows",
    )(x_send.reshape(experts, ROWS, model_width), dy_send.reshape(experts, ROWS, model_width),
      w_gate[0], w_up[0], w_down[0])

    x_rows = x_all.reshape(4 * chips * ROWS, model_width)
    dy_rows = dy_all.reshape(4 * chips * ROWS, model_width)
    reply, gate_out, d_gate_pre, d_up_pre, act = expert_backward(x_rows, dy_rows, f_gate, f_up, f_down)
    terms = [over_rows(left, right).astype(bf16).reshape(4, depth, half)
             for left, right in ((x_rows, d_gate_pre), (x_rows, d_up_pre), (dy_rows, act))]
    gates = jnp.broadcast_to(gate_out, (4 * chips * ROWS, 128))

    grad_shape = jax.ShapeDtypeStruct((depth, width), bf16)
    reply_out, gates_out, g_gate, g_up, g_down = pl.pallas_call(
        functools.partial(return_kernel, chips),
        out_shape=[jax.ShapeDtypeStruct((experts, ROWS, model_width), bf16),
                   jax.ShapeDtypeStruct((experts, ROWS, 128), jnp.float32)] + [grad_shape] * 3,
        in_specs=[anywhere] * 5,
        out_specs=[anywhere] * 5,
        scratch_shapes=[
            pltpu.VMEM((2, chips, ROWS, model_width), bf16), pltpu.VMEM((2, chips, ROWS, model_width), bf16),
            pltpu.VMEM((2, chips, ROWS, 128), jnp.float32), pltpu.VMEM((2, chips, ROWS, 128), jnp.float32),
            pltpu.VMEM((3, 2, depth, half), bf16), pltpu.VMEM((3, 2, depth, half), bf16),
            dma((8,)), dma((2,)), dma((2,)), dma((3, 2)), dma((3, 2)), dma((3, 2)), dma((3, 2)),
            dma((2, 2)), dma((2, 2))],
        compiler_params=pltpu.CompilerParams(has_side_effects=True, vmem_limit_bytes=48 << 20),
        name="return_rows",
    )(reply.reshape(2, 2, chips, ROWS, model_width), gates.reshape(2, 2, chips, ROWS, 128), *terms)

    token_grad = over_rows(dispatch_map, reply_out.reshape(buffer_rows, model_width)).astype(bf16)
    gate_rows = gates_out.reshape(buffer_rows, 128)[:, 0]
    gate_grad = jnp.stack([jnp.sum(jnp.where(pick, gate_rows[:, None], 0.0), axis=0) for pick in picks], axis=1)
    gate_grad = (gate_grad / gate_values.astype(jnp.float32)).astype(bf16)
    return token_grad, gate_grad, g_gate[None], g_up[None], g_down[None]


def solution(mesh):
    tokens_spec, weights_spec = P(("ep", "edp"), None), P("ep", "edp", None)
    return jax.shard_map(
        shards, mesh=mesh,
        in_specs=(tokens_spec,) * 4 + (weights_spec,) * 3,
        out_specs=(tokens_spec,) * 2 + (weights_spec,) * 3,
        check_vma=False,
    )
```

```python
import functools

import jax
import jax.numpy as jnp
from jax import lax
from jax.experimental import pallas as pl
from jax.experimental.pallas import tpu as pltpu
from jax.sharding import PartitionSpec as P

MESH = pl.DeviceIdType.MESH
ROWS = 16


def place():
    ep, plane = lax.axis_index("ep"), lax.axis_index("edp")
    core = lax.rem(ep, 2)
    parity = plane // 2
    beside = plane + 1 - 2 * lax.rem(plane, 2)
    across = 3 - plane
    return ep, ep // 2, core, plane, parity, beside, across


def remote(src, dst, send, recv, ep, plane):
    return pltpu.make_async_remote_copy(
        src_ref=src, dst_ref=dst, send_sem=send, recv_sem=recv,
        device_id=(ep, plane), device_id_type=MESH,
    )


def landed(ref, sem):
    pltpu.make_async_copy(ref, ref, sem).wait()


def layer_kernel(chips, x_send, dy_send, w_gate, w_up, w_down, reply_out, gates_out, g_gate, g_up, g_down,
                 x_all, dy_all, f_gate, f_up, f_down, slope, gated, act, d_gate, d_up, terms, arrived,
                 reply_in, gates_own, gates_in,
                 token_send, token_recv, hand_send, hand_recv, weight_send, weight_recv, relay_send,
                 sum_send, sum_recv, pass_send, pass_recv, out_send, out_recv, back_send, back_recv):
    ep, chip, core, plane, parity, beside, across = place()
    depth, width = w_gate.shape
    half = width // 2
    tile = min(half, 256)
    model_width = 4 * depth
    sibling = ep + 1 - 2 * core
    away = core != parity
    weights = (w_gate, w_up, w_down)
    fulls = (f_gate, f_up, f_down)
    grads = (g_gate, g_up, g_down)
    sends, alls = (x_send, dy_send), (x_all, dy_all)
    f32, bf16 = jnp.float32, jnp.bfloat16

    def rows_of(ref, shard):
        return ref.at[pl.ds(pl.multiple_of(shard * depth, 16), depth)]

    def columns(ref, part):
        return ref.at[:, pl.ds(pl.multiple_of(part * half, 128), half)]

    def block(ref, group, index):
        return ref.at[group, pl.ds(pl.multiple_of(index * ROWS, ROWS), ROWS)]

    for m in range(3):
        @pl.when(away)
        def _(m=m):
            for part in range(2):
                remote(columns(weights[m], part), rows_of(fulls[m], plane), weight_send.at[m, part],
                       weight_recv.at[m, 0], 2 * chip + part, across).start()

    for n in range(2):
        for group in range(2):
            def send(k, carry, n=n, group=group):
                to = lax.rem(chip + k, chips)
                to_plane = plane if group == 0 else across
                kind = parity if group == 0 else 1 - parity
                remote(sends[n].at[2 * to + kind], block(alls[n].at[core], group, chip), token_send.at[n, group],
                       token_recv.at[n, group], 2 * to + core, to_plane).start()
                return carry

            if group == 0:
                pltpu.make_async_copy(sends[n].at[2 * chip + parity], block(alls[n].at[core], 0, chip),
                                      token_recv.at[n, 0]).start()
            lax.fori_loop(1 if group == 0 else 0, chips, send, 0)
        if n == 0:
            for m in range(3):
                @pl.when(jnp.logical_not(away))
                def _(m=m):
                    for part in range(2):
                        remote(columns(weights[m], part), rows_of(fulls[m], plane), weight_send.at[m, part],
                               weight_recv.at[m, 1], 2 * chip + part, beside).start()
                    pltpu.make_async_copy(columns(weights[m], core), rows_of(fulls[m], plane),
                                          weight_recv.at[m, 2]).start()
                    remote(columns(weights[m], 1 - core), rows_of(fulls[m], plane), weight_send.at[m, 2],
                           weight_recv.at[m, 2], sibling, plane).start()

    def relay(m):
        return remote(rows_of(fulls[m], across), rows_of(fulls[m], across), relay_send.at[m],
                      weight_recv.at[m, 3], 2 * chip + core, beside)

    def hand_over(n, group):
        return remote(alls[n].at[core, group], alls[n].at[core, group], hand_send.at[n, group],
                      hand_recv.at[n, group], sibling, plane)

    def pass_on(n, group):
        landed(alls[n].at[core, group], token_recv.at[n, group])
        hand_over(n, group).start()

    def weights_here(m):
        landed(rows_of(fulls[m], beside), weight_recv.at[m, 1])
        landed(rows_of(fulls[m], plane), weight_recv.at[m, 2])
        landed(rows_of(fulls[m], 3 - beside), weight_recv.at[m, 3])

    def product(left, k, group, right, cols):
        deep = min(model_width, 512)
        total = None
        for at in range(0, model_width, deep):
            term = jnp.dot(left[k, group, :, at:at + deep], right[at:at + deep, cols], preferred_element_type=f32)
            total = term if total is None else total + term
        return total

    def tiles(n):
        return pl.ds(pl.multiple_of(n * tile, tile), tile)

    def forward(group):
        def step(i, carry):
            k, cols = i // (half // tile), tiles(lax.rem(i, half // tile))
            pre_gate = product(x_all, k, group, f_gate, cols)
            sigma = jax.nn.sigmoid(pre_gate)
            silu_val = pre_gate * sigma
            gated[k, group, :, cols] = silu_val
            slope[k, group, :, cols] = sigma * (1.0 + pre_gate * (1.0 - sigma))
            pre_up = product(x_all, k, group, f_up, cols)
            act[k, group, :, cols] = (gated[k, group, :, cols] * pre_up).astype(bf16)
            slope[k, group, :, cols] = slope[k, group, :, cols] * pre_up
            return carry

        lax.fori_loop(0, 2 * (half // tile), step, 0)

    def backward(k, group):
        gates_own[k, group] = jnp.zeros(gates_own.shape[2:], f32)

        def step(n, carry):
            cols = tiles(n)
            back = product(dy_all, k, group, f_down, cols)
            d_gate[k, group, :, cols] = (back * slope[k, group, :, cols]).astype(bf16)
            d_up[k, group, :, cols] = (back * gated[k, group, :, cols]).astype(bf16)
            part = jnp.sum(act[k, group, :, cols].astype(f32) * back, axis=1, keepdims=True)
            gates_own[k, group] = gates_own[k, group] + part
            return carry

        lax.fori_loop(0, half // tile, step, 0)

    relay_order = (0, 1)
    for m in relay_order:
        landed(rows_of(fulls[m], across), weight_recv.at[m, 0])
        relay(m).start()
    pass_on(0, 0)
    landed(rows_of(f_down, across), weight_recv.at[2, 0])
    relay(2).start()
    pass_on(0, 1)
    pass_on(1, 0)
    weights_here(0)
    weights_here(1)
    for group in range(2):
        landed(x_all.at[1 - core, group], hand_recv.at[0, group])
        forward(group)
    weights_here(2)
    backward(core, 0)
    landed(dy_all.at[1 - core, 0], hand_recv.at[1, 0])
    backward(1 - core, 0)
    pass_on(1, 1)
    backward(core, 1)
    landed(dy_all.at[1 - core, 1], hand_recv.at[1, 1])
    backward(1 - core, 1)

    def moved(m, i):
        return remote(terms.at[m, i], arrived.at[m, i], sum_send.at[m, i], sum_recv.at[m, i],
                      2 * chip + core, beside)

    def gradients(i, carry):
        shard = jnp.where(i == 0, 3 - beside, jnp.where(i == 1, beside, jnp.where(i == 2, across, plane)))
        cols = pl.ds(pl.multiple_of(shard * depth, 128), depth)
        over = (((0,), (0,)), ((), ()))

        def accumulate(m, left, right):
            def step(n, carry):
                total = None
                for k in range(2):
                    for group in range(2):
                        term = lax.dot_general(left[k, group, :, cols], right[k, group, :, tiles(n)], over,
                                               preferred_element_type=f32)
                        total = term if total is None else total + term
                terms[m, i, :, tiles(n)] = total.astype(bf16)
                return carry

            lax.fori_loop(0, half // tile, step, 0)

            @pl.when(i < 2)
            def _():
                moved(m, i).start()

        accumulate(0, x_all, d_gate)
        accumulate(1, x_all, d_up)
        accumulate(2, dy_all, act)
        return carry

    lax.fori_loop(0, 4, gradients, 0)

    for n in range(2):
        for group in range(2):
            hand_over(n, group).wait_send()

    def replies(k, group, other):
        wide = min(model_width, 512)

        def step(n, carry):
            cols = pl.ds(pl.multiple_of(n * wide, wide), wide)
            contract = (((1,), (1,)), ((), ()))
            total = lax.dot_general(d_gate[k, group], f_gate[cols], contract, preferred_element_type=f32)
            total = total + lax.dot_general(d_up[k, group], f_up[cols], contract, preferred_element_type=f32)
            if other is not None:
                total = total + other[group, :, cols].astype(f32)
            x_all[k, group, :, cols] = total.astype(bf16)
            return carry

        lax.fori_loop(0, model_width // wide, step, 0)

    gates_pass = remote(gates_own.at[1 - core], gates_in, pass_send.at[2], pass_recv.at[2], sibling, plane)
    gates_pass.start()

    def reply_pass(group):
        return remote(x_all.at[1 - core, group], reply_in.at[group], pass_send.at[group], pass_recv.at[group],
                      sibling, plane)

    for group in (1, 0):
        replies(1 - core, group, None)
        reply_pass(group).start()
    gates_pass.wait()
    gates_own[core] = gates_own[core] + gates_in[...]
    for group in (1, 0):
        reply_pass(group).wait()
        replies(core, group, reply_in)

        def send(k, carry, group=group):
            to = lax.rem(chip + k, chips)
            to_plane = plane if group == 0 else across
            remote(block(x_all.at[core], group, to), reply_out.at[2 * chip + parity], back_send.at[0, group],
                   back_recv.at[0, group], 2 * to + core, to_plane).start()
            remote(block(gates_own.at[core], group, to), gates_out.at[2 * chip + parity], back_send.at[1, group],
                   back_recv.at[1, group], 2 * to + core, to_plane).start()
            return carry

        if group == 0:
            pltpu.make_async_copy(block(x_all.at[core], 0, chip), reply_out.at[2 * chip + parity],
                                  back_recv.at[0, 0]).start()
            pltpu.make_async_copy(block(gates_own.at[core], 0, chip), gates_out.at[2 * chip + parity],
                                  back_recv.at[1, 0]).start()
        lax.fori_loop(1 if group == 0 else 0, chips, send, 0)

    for i in range(2):
        for m in range(3):
            moved(m, i).wait()
            step = 128

            def add(k, carry, m=m, i=i):
                rows = pl.ds(pl.multiple_of(k * step, step), step)
                total = terms[m, 2 + i, rows].astype(f32) + arrived[m, i, rows].astype(f32)
                terms[m, 2 + i, rows] = total.astype(bf16)
                return carry

            lax.fori_loop(0, depth // step, add, 0)
            if i == 0:
                remote(terms.at[m, 2], columns(grads[m], core), out_send.at[m, 0], out_recv.at[m, core],
                       2 * chip + parity, across).start()
            else:
                @pl.when(core == parity)
                def _(m=m):
                    pltpu.make_async_copy(terms.at[m, 3], columns(grads[m], core), out_recv.at[m, core]).start()

                @pl.when(core != parity)
                def _(m=m):
                    remote(terms.at[m, 3], columns(grads[m], core), out_send.at[m, 1], out_recv.at[m, core],
                           2 * chip + parity, plane).start()

    for m in range(3):
        relay(m).wait_send()
        for part in range(2):
            landed(columns(weights[m], part), weight_send.at[m, part])

        @pl.when(jnp.logical_not(away))
        def _(m=m):
            landed(columns(weights[m], 0), weight_send.at[m, 2])
        landed(terms.at[m, 2], out_send.at[m, 0])

        @pl.when(core != parity)
        def _(m=m):
            landed(terms.at[m, 3], out_send.at[m, 1])
        for part in range(2):
            landed(columns(grads[m], part), out_recv.at[m, part])
    sent = pl.ds(0, (chips - 1) * ROWS)
    for n in range(2):
        landed(alls[n].at[core, 0, sent], token_send.at[n, 0])
        landed(alls[n].at[core, 1], token_send.at[n, 1])
    for n, own in enumerate((x_all, gates_own)):
        landed(own.at[core, 0, sent], back_send.at[n, 0])
        landed(own.at[core, 1], back_send.at[n, 1])
        for group in range(2):
            landed(own.at[core, group], back_recv.at[n, group])


def over_rows(left, right):
    return lax.dot_general(left, right, (((0,), (0,)), ((), ())), preferred_element_type=jnp.float32)


def shards(tokens, upstream, expert_ids, gate_values, w_gate, w_up, w_down):
    experts = lax.axis_size("ep")
    chips = experts // 2
    tok_count, top_count = expert_ids.shape
    model_width = tokens.shape[1]
    depth, width = w_gate.shape[1:]
    half = width // 2
    buffer_rows = experts * ROWS
    bf16 = jnp.bfloat16
    flat_ids = expert_ids.reshape(-1)
    onehot = (flat_ids[:, None] == jnp.arange(experts, dtype=jnp.int32)[None, :]).astype(jnp.int32)
    slot_idx = jnp.sum(jnp.cumsum(onehot, axis=0) * onehot, axis=1) - 1
    target = (flat_ids * ROWS + slot_idx).reshape(tok_count, top_count)
    slots = jnp.arange(buffer_rows, dtype=jnp.int32)
    picks = [slots[:, None] == target[None, :, k] for k in range(top_count)]
    zero = jnp.zeros((), bf16)
    dispatch_map = sum(pick.astype(bf16) for pick in picks)
    scaled_map = sum(jnp.where(pick, gate_values[None, :, k], zero) for k, pick in enumerate(picks))
    x_send = jnp.dot(dispatch_map, tokens, preferred_element_type=jnp.float32).astype(bf16)
    dy_send = jnp.dot(scaled_map, upstream, preferred_element_type=jnp.float32).astype(bf16)

    anywhere = pl.BlockSpec(memory_space=pl.ANY)
    dma = pltpu.SemaphoreType.DMA
    tall = chips * ROWS
    rows_buffer = pltpu.VMEM((2, 2, tall, model_width), bf16)
    full_buffer = pltpu.VMEM((4 * depth, half), bf16)
    wide_buffer = pltpu.VMEM((2, 2, tall, half), jnp.float32)
    narrow_buffer = pltpu.VMEM((2, 2, tall, half), bf16)
    grad_shape = jax.ShapeDtypeStruct((depth, width), bf16)
    reply_out, gates_out, g_gate, g_up, g_down = pl.pallas_call(
        functools.partial(layer_kernel, chips),
        out_shape=[jax.ShapeDtypeStruct((experts, ROWS, model_width), bf16),
                   jax.ShapeDtypeStruct((experts, ROWS, 128), jnp.float32)] + [grad_shape] * 3,
        in_specs=[anywhere] * 5,
        out_specs=[anywhere] * 5,
        scratch_shapes=[
            rows_buffer, rows_buffer, full_buffer, full_buffer, full_buffer,
            wide_buffer, wide_buffer, narrow_buffer, narrow_buffer, narrow_buffer,
            pltpu.VMEM((3, 4, depth, half), bf16), pltpu.VMEM((3, 2, depth, half), bf16),
            pltpu.VMEM((2, tall, model_width), bf16),
            pltpu.VMEM((2, 2, tall, 128), jnp.float32), pltpu.VMEM((2, tall, 128), jnp.float32),
            dma((2, 2)), dma((2, 2)), dma((2, 2)), dma((2, 2)), dma((3, 3)), dma((3, 4)), dma((3,)),
            dma((3, 2)), dma((3, 2)), dma((3,)), dma((3,)), dma((3, 2)), dma((3, 2)), dma((2, 2)), dma((2, 2))],
        compiler_params=pltpu.CompilerParams(has_side_effects=True, vmem_limit_bytes=60 << 20),
        name="expert_layer",
    )(x_send.reshape(experts, ROWS, model_width), dy_send.reshape(experts, ROWS, model_width),
      w_gate[0], w_up[0], w_down[0])

    token_grad = over_rows(dispatch_map, reply_out.reshape(buffer_rows, model_width)).astype(bf16)
    gate_rows = gates_out.reshape(buffer_rows, 128)[:, 0]
    gate_grad = jnp.stack([jnp.sum(jnp.where(pick, gate_rows[:, None], 0.0), axis=0) for pick in picks], axis=1)
    gate_grad = (gate_grad / gate_values.astype(jnp.float32)).astype(bf16)
    return token_grad, gate_grad, g_gate[None], g_up[None], g_down[None]


def solution(mesh):
    tokens_spec, weights_spec = P(("ep", "edp"), None), P("ep", "edp", None)
    return jax.shard_map(
        shards, mesh=mesh,
        in_specs=(tokens_spec,) * 4 + (weights_spec,) * 3,
        out_specs=(tokens_spec,) * 2 + (weights_spec,) * 3,
        check_vma=False,
    )
```

```python
import functools

import jax
import jax.numpy as jnp
from jax import lax
from jax.experimental import pallas as pl
from jax.experimental.pallas import tpu as pltpu
from jax.sharding import PartitionSpec as P

MESH = pl.DeviceIdType.MESH
ROWS = 16


def place():
    ep, plane = lax.axis_index("ep"), lax.axis_index("edp")
    core = lax.rem(ep, 2)
    parity = plane // 2
    beside = plane + 1 - 2 * lax.rem(plane, 2)
    across = 3 - plane
    return ep, ep // 2, core, plane, parity, beside, across


def remote(src, dst, send, recv, ep, plane):
    return pltpu.make_async_remote_copy(
        src_ref=src, dst_ref=dst, send_sem=send, recv_sem=recv,
        device_id=(ep, plane), device_id_type=MESH,
    )


def landed(ref, sem):
    pltpu.make_async_copy(ref, ref, sem).wait()


def layer_kernel(chips, tokens, upstream, info_own, w_gate, w_up, w_down,
                 mix_own, mix_across, gates_out, gates_across, g_gate, g_up, g_down,
                 x_all, dy_all, f_gate, f_up, f_down, slope, gated, act, d_gate, d_up, terms, arrived,
                 x_stage, dy_stage, gates_own, gates_in, gates_back, gates_mix, info_in,
                 load_sem, swap_send, swap_recv, info_sem, stay_sem,
                 token_send, token_recv, hand_send, hand_recv, weight_send, weight_recv, relay_send,
                 sum_send, sum_recv, pass_send, pass_recv, out_send, out_recv, back_send, back_recv,
                 mix_send, mix_recv):
    ep, chip, core, plane, parity, beside, across = place()
    depth, width = w_gate.shape
    half = width // 2
    tile = min(half, 256)
    tok_count, model_width = tokens.shape
    tall = chips * ROWS
    sibling = ep + 1 - 2 * core
    away = core != parity
    weights = (w_gate, w_up, w_down)
    fulls = (f_gate, f_up, f_down)
    grads = (g_gate, g_up, g_down)
    stages, alls = (x_stage, dy_stage), (x_all, dy_all)
    reply_back, reply_in = x_stage, dy_stage
    f32, bf16 = jnp.float32, jnp.bfloat16

    def rows_of(ref, shard):
        return ref.at[pl.ds(pl.multiple_of(shard * depth, 16), depth)]

    def columns(ref, part):
        return ref.at[:, pl.ds(pl.multiple_of(part * half, 128), half)]

    def block(ref, group, index):
        return ref.at[group, pl.ds(pl.multiple_of(index * ROWS, ROWS), ROWS)]

    chunks = model_width // half
    fit = depth // tok_count
    slabs = -(-chunks // fit)

    def chunk_of(n, group, j):
        slab = slabs * (2 * n + group) + j // fit
        return terms.at[slab // 4, slab % 4, pl.ds(j % fit * tok_count, tok_count)]

    def source_of(n, j):
        return (tokens, upstream)[n].at[:, pl.ds(j * half, half)]

    def loads(n):
        return [pltpu.make_async_copy(source_of(n, j), chunk_of(n, 0, j), load_sem.at[n, j]) for j in range(chunks)]

    def swaps(n):
        return [remote(source_of(n, j), chunk_of(n, 1, j), swap_send.at[n, j], swap_recv.at[n, j], ep, across)
                for j in range(chunks)]

    def info_swap():
        return remote(info_own, info_in, info_sem.at[0], info_sem.at[1], ep, across)

    def hits(group):
        info = info_own if group == 0 else info_in
        rows = lax.broadcasted_iota(jnp.int32, (tall, tok_count), 0)
        slot = (rows + (rows // ROWS + parity) * ROWS).astype(f32)
        return [slot == info[k:k + 1, :tok_count] for k in range(2)]

    def picks(n, group):
        info = info_own if group == 0 else info_in
        levels = [info[2 + k:3 + k, :tok_count] if n else jnp.ones((1, tok_count), f32) for k in range(2)]
        terms_of = [jnp.where(hit, level, 0.0) for hit, level in zip(hits(group), levels)]
        return (terms_of[0] + terms_of[1]).astype(bf16)

    def dispatch(n, group):
        chosen = picks(n, group)
        for j in range(chunks):
            rows = jnp.dot(chosen, chunk_of(n, group, j)[...], preferred_element_type=f32)
            stages[n][group, :, j * half:(j + 1) * half] = rows.astype(bf16)

    def stays(n, group):
        return pltpu.make_async_copy(block(stages[n], group, chip), block(alls[n].at[core], group, chip),
                                     stay_sem.at[n, group])

    def spread(n, group):
        def send(k, carry):
            to = lax.rem(chip + k, chips)
            remote(block(stages[n], group, to), block(alls[n].at[core], group, chip), token_send.at[n, group],
                   token_recv.at[n, group], 2 * to + core, plane).start()
            return carry

        stays(n, group).start()
        lax.fori_loop(1, chips, send, 0)

    def spread_done(n, group):
        stays(n, group).wait()
        landed(stages[n].at[group, pl.ds(0, (chips - 1) * ROWS)], token_send.at[n, group])

    def away_weights(m):
        @pl.when(away)
        def _():
            for part in range(2):
                remote(columns(weights[m], part), rows_of(fulls[m], plane), weight_send.at[m, part],
                       weight_recv.at[m, 0], 2 * chip + part, across).start()

    def home_weights(m):
        @pl.when(jnp.logical_not(away))
        def _():
            for part in range(2):
                remote(columns(weights[m], part), rows_of(fulls[m], plane), weight_send.at[m, part],
                       weight_recv.at[m, 1], 2 * chip + part, beside).start()
            pltpu.make_async_copy(columns(weights[m], core), rows_of(fulls[m], plane),
                                  weight_recv.at[m, 2]).start()
            remote(columns(weights[m], 1 - core), rows_of(fulls[m], plane), weight_send.at[m, 2],
                   weight_recv.at[m, 2], sibling, plane).start()

    for n in range(2):
        for copy in loads(n):
            copy.start()
    barrier = pltpu.get_barrier_semaphore()

    def greet(k, carry):
        pl.semaphore_signal(barrier, inc=1, device_id=(2 * lax.rem(chip + k, chips) + core, plane),
                            device_id_type=MESH)
        return carry

    lax.fori_loop(1, chips, greet, 0)
    for other in ((sibling, plane), (ep, across), (sibling, across), (ep, beside), (sibling, beside)):
        pl.semaphore_signal(barrier, inc=1, device_id=other, device_id_type=MESH)
    for copy in loads(0):
        copy.wait()
    dispatch(0, 0)
    pl.semaphore_wait(barrier, chips + 4)

    info_swap().start()
    for copy in swaps(0):
        copy.start()
    away_weights(0)
    for m in range(3):
        home_weights(m)
    for copy in swaps(1):
        copy.start()
    away_weights(1)
    away_weights(2)
    spread(0, 0)
    for copy in loads(1):
        copy.wait()
    dispatch(1, 0)
    spread(1, 0)

    def relay(m):
        return remote(rows_of(fulls[m], across), rows_of(fulls[m], across), relay_send.at[m],
                      weight_recv.at[m, 3], 2 * chip + core, beside)

    def hand_over(n, group):
        return remote(alls[n].at[core, group], alls[n].at[core, group], hand_send.at[n, group],
                      hand_recv.at[n, group], sibling, plane)

    def pass_on(n, group):
        landed(alls[n].at[core, group, pl.ds(0, (chips - 1) * ROWS)], token_recv.at[n, group])
        spread_done(n, group)
        hand_over(n, group).start()

    def weights_here(m):
        landed(rows_of(fulls[m], beside), weight_recv.at[m, 1])
        landed(rows_of(fulls[m], plane), weight_recv.at[m, 2])
        landed(rows_of(fulls[m], 3 - beside), weight_recv.at[m, 3])

    def product(left, k, group, right, cols):
        deep = min(model_width, 512)
        total = None
        for at in range(0, model_width, deep):
            term = jnp.dot(left[k, group, :, at:at + deep], right[at:at + deep, cols], preferred_element_type=f32)
            total = term if total is None else total + term
        return total

    def tiles(n):
        return pl.ds(pl.multiple_of(n * tile, tile), tile)

    def forward(group):
        def step(i, carry):
            k, cols = i // (half // tile), tiles(lax.rem(i, half // tile))
            pre_gate = product(x_all, k, group, f_gate, cols)
            sigma = jax.nn.sigmoid(pre_gate)
            silu_val = pre_gate * sigma
            gated[k, group, :, cols] = silu_val
            slope[k, group, :, cols] = sigma * (1.0 + pre_gate * (1.0 - sigma))
            pre_up = product(x_all, k, group, f_up, cols)
            act[k, group, :, cols] = (gated[k, group, :, cols] * pre_up).astype(bf16)
            slope[k, group, :, cols] = slope[k, group, :, cols] * pre_up
            return carry

        lax.fori_loop(0, 2 * (half // tile), step, 0)

    def backward(k, group):
        gates_own[k, group] = jnp.zeros(gates_own.shape[2:], f32)

        def step(n, carry):
            cols = tiles(n)
            back = product(dy_all, k, group, f_down, cols)
            d_gate[k, group, :, cols] = (back * slope[k, group, :, cols]).astype(bf16)
            d_up[k, group, :, cols] = (back * gated[k, group, :, cols]).astype(bf16)
            part = jnp.sum(act[k, group, :, cols].astype(f32) * back, axis=1, keepdims=True)
            gates_own[k, group] = gates_own[k, group] + part
            return carry

        lax.fori_loop(0, half // tile, step, 0)

    def start_relay(m):
        landed(rows_of(fulls[m], across), weight_recv.at[m, 0])
        relay(m).start()

    info_swap().wait()
    for copy in swaps(0):
        copy.wait_recv()
    dispatch(0, 1)
    spread(0, 1)
    start_relay(0)
    pass_on(0, 0)
    for copy in swaps(1):
        copy.wait_recv()
    dispatch(1, 1)
    pass_on(0, 1)
    spread(1, 1)
    pass_on(1, 0)
    start_relay(1)
    pass_on(1, 1)
    weights_here(0)
    weights_here(1)
    landed(x_all.at[1 - core, 0], hand_recv.at[0, 0])
    forward(0)
    start_relay(2)
    landed(x_all.at[1 - core, 1], hand_recv.at[0, 1])
    forward(1)
    weights_here(2)
    for group in range(2):
        landed(dy_all.at[1 - core, group], hand_recv.at[1, group])
        backward(core, group)
        backward(1 - core, group)

    def moved(m, i):
        return remote(terms.at[m, i], arrived.at[m, i], sum_send.at[m, i], sum_recv.at[m, i],
                      2 * chip + core, beside)

    def gradients(i, carry):
        shard = jnp.where(i == 0, 3 - beside, jnp.where(i == 1, beside, jnp.where(i == 2, across, plane)))
        cols = pl.ds(pl.multiple_of(shard * depth, 128), depth)
        over = (((0,), (0,)), ((), ()))

        def accumulate(m, left, right):
            def step(n, carry):
                total = None
                for k in range(2):
                    for group in range(2):
                        term = lax.dot_general(left[k, group, :, cols], right[k, group, :, tiles(n)], over,
                                               preferred_element_type=f32)
                        total = term if total is None else total + term
                terms[m, i, :, tiles(n)] = total.astype(bf16)
                return carry

            lax.fori_loop(0, half // tile, step, 0)

            @pl.when(i < 2)
            def _():
                moved(m, i).start()

        accumulate(0, x_all, d_gate)
        accumulate(1, x_all, d_up)
        accumulate(2, dy_all, act)
        return carry

    lax.fori_loop(0, 4, gradients, 0)

    for n in range(2):
        for group in range(2):
            hand_over(n, group).wait_send()

    def replies(k, group, other):
        wide = min(model_width, 512)

        def step(n, carry):
            cols = pl.ds(pl.multiple_of(n * wide, wide), wide)
            contract = (((1,), (1,)), ((), ()))
            total = lax.dot_general(d_gate[k, group], f_gate[cols], contract, preferred_element_type=f32)
            total = total + lax.dot_general(d_up[k, group], f_up[cols], contract, preferred_element_type=f32)
            if other is not None:
                total = total + other[group, :, cols].astype(f32)
            x_all[k, group, :, cols] = total.astype(bf16)
            return carry

        lax.fori_loop(0, model_width // wide, step, 0)

    gates_pass = remote(gates_own.at[1 - core], gates_in, pass_send.at[2], pass_recv.at[2], sibling, plane)
    gates_pass.start()

    def reply_pass(group):
        return remote(x_all.at[1 - core, group], reply_in.at[group], pass_send.at[group], pass_recv.at[group],
                      sibling, plane)

    for group in (1, 0):
        replies(1 - core, group, None)
        reply_pass(group).start()
    gates_pass.wait()
    gates_own[core] = gates_own[core] + gates_in[...]
    for group in (1, 0):
        reply_pass(group).wait()
        replies(core, group, reply_in)

        def send(k, carry, group=group):
            to = lax.rem(chip + k, chips)
            for n, (own, back) in enumerate(((x_all, reply_back), (gates_own, gates_back))):
                remote(block(own.at[core], group, to), block(back, group, chip), back_send.at[n, group],
                       back_recv.at[n, group], 2 * to + core, plane).start()
            return carry

        for n, (own, back) in enumerate(((x_all, reply_back), (gates_own, gates_back))):
            pltpu.make_async_copy(block(own.at[core], group, chip), block(back, group, chip),
                                  back_recv.at[n, group]).start()
        lax.fori_loop(1, chips, send, 0)

    def combine(group):
        landed(reply_back.at[group], back_recv.at[0, group])
        landed(gates_back.at[group], back_recv.at[1, group])
        chosen = picks(0, group)
        for j in range(chunks):
            cols = slice(j * half, (j + 1) * half)
            total = lax.dot_general(chosen, reply_back[group, :, cols], (((0,), (0,)), ((), ())),
                                    preferred_element_type=f32)
            dy_all[0, group, 0:tok_count, cols] = total.astype(bf16)
        gates_mix[group] = jnp.zeros(gates_mix.shape[1:], f32)
        for k, hit in enumerate(hits(group)):
            values = jnp.where(hit, gates_back[group, :, 0:1], 0.0)
            gates_mix[group, k:k + 1, 0:tok_count] = jnp.sum(values, axis=0, keepdims=True)

    def mixed(group):
        rows = dy_all.at[0, group, pl.ds(0, tok_count)]
        if group == 0:
            return [pltpu.make_async_copy(rows, mix_own, mix_send.at[0, 0]),
                    pltpu.make_async_copy(gates_mix.at[0], gates_out, mix_send.at[0, 1])]
        return [remote(rows, mix_across, mix_send.at[1, 0], mix_recv.at[0], ep, across),
                remote(gates_mix.at[1], gates_across, mix_send.at[1, 1], mix_recv.at[1], ep, across)]

    for i in range(2):
        if i == 1:
            for group in (1, 0):
                combine(group)
                for copy in mixed(group):
                    copy.start()
        for m in range(3):
            moved(m, i).wait()
            step = 128

            def add(k, carry, m=m, i=i):
                rows = pl.ds(pl.multiple_of(k * step, step), step)
                total = terms[m, 2 + i, rows].astype(f32) + arrived[m, i, rows].astype(f32)
                terms[m, 2 + i, rows] = total.astype(bf16)
                return carry

            lax.fori_loop(0, depth // step, add, 0)
            if i == 0:
                remote(terms.at[m, 2], columns(grads[m], core), out_send.at[m, 0], out_recv.at[m, core],
                       2 * chip + parity, across).start()
            else:
                @pl.when(core == parity)
                def _(m=m):
                    pltpu.make_async_copy(terms.at[m, 3], columns(grads[m], core), out_recv.at[m, core]).start()

                @pl.when(core != parity)
                def _(m=m):
                    remote(terms.at[m, 3], columns(grads[m], core), out_send.at[m, 1], out_recv.at[m, core],
                           2 * chip + parity, plane).start()

    for m in range(3):
        relay(m).wait_send()
        for part in range(2):
            landed(columns(weights[m], part), weight_send.at[m, part])

        @pl.when(jnp.logical_not(away))
        def _(m=m):
            landed(columns(weights[m], 0), weight_send.at[m, 2])
        landed(terms.at[m, 2], out_send.at[m, 0])

        @pl.when(core != parity)
        def _(m=m):
            landed(terms.at[m, 3], out_send.at[m, 1])
        for part in range(2):
            landed(columns(grads[m], part), out_recv.at[m, part])
    for n in range(2):
        for copy in swaps(n):
            copy.wait_send()
    for n, own in enumerate((x_all, gates_own)):
        for group in range(2):
            landed(own.at[core, group, pl.ds(0, (chips - 1) * ROWS)], back_send.at[n, group])
    for group in range(2):
        for copy in mixed(group):
            copy.wait()


def shards(tokens, upstream, expert_ids, gate_values, w_gate, w_up, w_down):
    experts = lax.axis_size("ep")
    chips = experts // 2
    tok_count, top_count = expert_ids.shape
    model_width = tokens.shape[1]
    depth, width = w_gate.shape[1:]
    half = width // 2
    bf16 = jnp.bfloat16
    flat_ids = expert_ids.reshape(-1)
    onehot = (flat_ids[:, None] == jnp.arange(experts, dtype=jnp.int32)[None, :]).astype(jnp.int32)
    slot_idx = jnp.sum(jnp.cumsum(onehot, axis=0) * onehot, axis=1) - 1
    target = (flat_ids * ROWS + slot_idx).reshape(tok_count, top_count)
    lines = jnp.concatenate([target.astype(jnp.float32), gate_values.astype(jnp.float32)], axis=1)
    lanes = -(-tok_count // 128) * 128
    info = jnp.pad(lines.T, ((0, 4), (0, lanes - tok_count)))

    anywhere = pl.BlockSpec(memory_space=pl.ANY)
    dma = pltpu.SemaphoreType.DMA
    tall = chips * ROWS
    rows_buffer = pltpu.VMEM((2, 2, tall, model_width), bf16)
    full_buffer = pltpu.VMEM((4 * depth, half), bf16)
    wide_buffer = pltpu.VMEM((2, 2, tall, half), jnp.float32)
    narrow_buffer = pltpu.VMEM((2, 2, tall, half), bf16)
    grad_shape = jax.ShapeDtypeStruct((depth, width), bf16)
    mix_shape = jax.ShapeDtypeStruct((tok_count, model_width), bf16)
    info_shape = jax.ShapeDtypeStruct(info.shape, jnp.float32)
    mix_own, mix_across, gates_own, gates_across, g_gate, g_up, g_down = pl.pallas_call(
        functools.partial(layer_kernel, chips),
        out_shape=[mix_shape] * 2 + [info_shape] * 2 + [grad_shape] * 3,
        in_specs=[anywhere] * 2 + [pl.BlockSpec(memory_space=pltpu.VMEM)] + [anywhere] * 3,
        out_specs=[anywhere] * 7,
        scratch_shapes=[
            rows_buffer, rows_buffer, full_buffer, full_buffer, full_buffer,
            wide_buffer, wide_buffer, narrow_buffer, narrow_buffer, narrow_buffer,
            pltpu.VMEM((3, 4, depth, half), bf16), pltpu.VMEM((3, 2, depth, half), bf16),
            pltpu.VMEM((2, tall, model_width), bf16), pltpu.VMEM((2, tall, model_width), bf16),
            pltpu.VMEM((2, 2, tall, 128), jnp.float32), pltpu.VMEM((2, tall, 128), jnp.float32),
            pltpu.VMEM((2, tall, 128), jnp.float32), pltpu.VMEM((2, 8, lanes), jnp.float32),
            pltpu.VMEM((8, lanes), jnp.float32),
            dma((2, model_width // half)), dma((2, model_width // half)), dma((2, model_width // half)),
            dma((2,)), dma((2, 2)),
            dma((2, 2)), dma((2, 2)), dma((2, 2)), dma((2, 2)), dma((3, 3)), dma((3, 4)), dma((3,)),
            dma((3, 2)), dma((3, 2)), dma((3,)), dma((3,)), dma((3, 2)), dma((3, 2)), dma((2, 2)), dma((2, 2)),
            dma((2, 2)), dma((2,))],
        compiler_params=pltpu.CompilerParams(has_side_effects=True, collective_id=0, vmem_limit_bytes=60 << 20),
        name="expert_layer",
    )(tokens, upstream, info, w_gate[0], w_up[0], w_down[0])

    token_grad = (mix_own.astype(jnp.float32) + mix_across.astype(jnp.float32)).astype(bf16)
    gate_grad = (gates_own + gates_across)[:top_count, :tok_count].T
    gate_grad = (gate_grad / gate_values.astype(jnp.float32)).astype(bf16)
    return token_grad, gate_grad, g_gate[None], g_up[None], g_down[None]


def solution(mesh):
    tokens_spec, weights_spec = P(("ep", "edp"), None), P("ep", "edp", None)
    return jax.shard_map(
        shards, mesh=mesh,
        in_specs=(tokens_spec,) * 4 + (weights_spec,) * 3,
        out_specs=(tokens_spec,) * 2 + (weights_spec,) * 3,
        check_vma=False,
    )
```

```python
import functools

import jax
import jax.numpy as jnp
from jax import lax
from jax.experimental import pallas as pl
from jax.experimental.pallas import tpu as pltpu
from jax.sharding import PartitionSpec as P

MESH = pl.DeviceIdType.MESH
ROWS = 16
PIECES = 1


def place():
    ep, plane = lax.axis_index("ep"), lax.axis_index("edp")
    core = lax.rem(ep, 2)
    parity = plane // 2
    beside = plane + 1 - 2 * lax.rem(plane, 2)
    across = 3 - plane
    return ep, ep // 2, core, plane, parity, beside, across


def remote(src, dst, send, recv, ep, plane):
    return pltpu.make_async_remote_copy(
        src_ref=src, dst_ref=dst, send_sem=send, recv_sem=recv,
        device_id=(ep, plane), device_id_type=MESH,
    )


def landed(ref, sem):
    pltpu.make_async_copy(ref, ref, sem).wait()


def layer_kernel(chips, tokens, upstream, ids_own, levels_own, w_gate, w_up, w_down,
                 token_out, gates_out, g_all,
                 x_all, dy_all, f_gate, f_up, f_down, slope, gated, act, d_gate, d_up, terms, arrived,
                 x_stage, dy_stage, gates_own, gates_in, gates_back, gates_mix, info_own, info_in,
                 mix_in, gates_mixed,
                 load_sem, swap_send, swap_recv, info_sem, stay_sem,
                 token_send, token_recv, hand_send, hand_recv, weight_send, weight_recv, away_recv, relay_send,
                 sum_send, sum_recv, pass_send, pass_recv, out_send, out_recv, back_send, back_recv,
                 mix_send, mix_recv):
    ep, chip, core, plane, parity, beside, across = place()
    depth, width = w_gate.shape
    half = width // 2
    tile = min(half, 256)
    parts = half // tile
    tok_count, model_width = tokens.shape
    tall = chips * ROWS
    sibling = ep + 1 - 2 * core
    away = core != parity
    weights = (w_gate, w_up, w_down)
    fulls = (f_gate, f_up, f_down)
    grads = [g_all.at[m] for m in range(3)]
    stages, alls = (x_stage, dy_stage), (x_all, dy_all)
    reply_back, reply_in = x_stage, dy_stage
    f32, bf16 = jnp.float32, jnp.bfloat16

    def rows_of(ref, shard):
        return ref.at[pl.ds(pl.multiple_of(shard * depth, 16), depth)]

    def columns(ref, part):
        return ref.at[:, pl.ds(pl.multiple_of(part * half, 128), half)]

    def strip(ref, part, n):
        return ref.at[:, pl.ds(pl.multiple_of(part * half + n * tile, 128), tile)]

    def shard_strip(m, shard, n):
        return strip(rows_of(fulls[m], shard), 0, n)

    def block(ref, group, index):
        return ref.at[group, pl.ds(pl.multiple_of(index * ROWS, ROWS), ROWS)]

    chunks = model_width // half
    fit = depth // tok_count
    slabs = -(-chunks // fit)

    def chunk_of(n, group, j):
        slab = slabs * (2 * n + group) + j // fit
        return terms.at[slab // 4, slab % 4, pl.ds(j % fit * tok_count, tok_count)]

    def source_of(n, j):
        return (tokens, upstream)[n].at[:, pl.ds(j * half, half)]

    def loads(n):
        return [pltpu.make_async_copy(source_of(n, j), chunk_of(n, 0, j), load_sem.at[n, j]) for j in range(chunks)]

    def swaps(n):
        return [remote(source_of(n, j), chunk_of(n, 1, j), swap_send.at[n, j], swap_recv.at[n, j], ep, across)
                for j in range(chunks)]

    def info_swap():
        return remote(info_own, info_in, info_sem.at[0], info_sem.at[1], ep, across)

    def hits(group):
        info = info_own if group == 0 else info_in
        ids = [info[k:k + 1, :tok_count] for k in range(2)]
        names = lax.broadcasted_iota(jnp.int32, (2 * chips, tok_count), 0).astype(f32)
        named = [names == one for one in ids]
        ones = [jnp.where(one, 1.0, 0.0) for one in named]
        earlier = (lax.broadcasted_iota(jnp.int32, (tok_count, tok_count), 0)
                   < lax.broadcasted_iota(jnp.int32, (tok_count, tok_count), 1))
        ranks = jnp.dot((ones[0] + ones[1]).astype(bf16), jnp.where(earlier, 1.0, 0.0).astype(bf16),
                        preferred_element_type=f32)
        rows = lax.broadcasted_iota(jnp.int32, (tall, tok_count), 0)
        slot = (rows + (rows // ROWS + parity) * ROWS).astype(f32)
        return [slot == ids[k] * ROWS + jnp.sum(ones[k] * ranks, axis=0, keepdims=True) for k in range(2)]

    def picks(n, group):
        info = info_own if group == 0 else info_in
        levels = [info[2 + k:3 + k, :tok_count] if n else jnp.ones((1, tok_count), f32) for k in range(2)]
        terms_of = [jnp.where(hit, level, 0.0) for hit, level in zip(hits(group), levels)]
        return (terms_of[0] + terms_of[1]).astype(bf16)

    def dispatch(n, group):
        chosen = picks(n, group)
        for j in range(chunks):
            rows = jnp.dot(chosen, chunk_of(n, group, j)[...], preferred_element_type=f32)
            stages[n][group, :, j * half:(j + 1) * half] = rows.astype(bf16)

    def stays(n, group):
        return pltpu.make_async_copy(block(stages[n], group, chip), block(alls[n].at[core], group, chip),
                                     stay_sem.at[n, group])

    def spread(n, group):
        def send(k, carry):
            to = lax.rem(chip + k, chips)
            remote(block(stages[n], group, to), block(alls[n].at[core], group, chip), token_send.at[n, group],
                   token_recv.at[n, group], 2 * to + core, plane).start()
            return carry

        stays(n, group).start()
        lax.fori_loop(1, chips, send, 0)

    def spread_done(n, group):
        stays(n, group).wait()
        landed(stages[n].at[group, pl.ds(0, (chips - 1) * ROWS)], token_send.at[n, group])

    size = depth // PIECES

    def piece(m, shard, n, r):
        return strip(fulls[m].at[pl.ds(pl.multiple_of(shard * depth + r * size, 16), size)], 0, n)

    def away_weights(m, n):
        @pl.when(away)
        def _():
            for part in range(2):
                for r in range(PIECES):
                    remote(strip(weights[m].at[pl.ds(r * size, size)], part, n), piece(m, plane, n, r),
                           weight_send.at[m, n, part], away_recv.at[m, n, r], 2 * chip + part, across).start()

    def home_weights(m, n):
        @pl.when(jnp.logical_not(away))
        def _():
            for part in range(2):
                remote(strip(weights[m], part, n), shard_strip(m, plane, n), weight_send.at[m, n, part],
                       weight_recv.at[m, n, 1], 2 * chip + part, beside).start()
            pltpu.make_async_copy(strip(weights[m], core, n), shard_strip(m, plane, n),
                                  weight_recv.at[m, n, 2]).start()
            remote(strip(weights[m], 1 - core, n), shard_strip(m, plane, n), weight_send.at[m, n, 2],
                   weight_recv.at[m, n, 2], sibling, plane).start()

    for n in range(2):
        for copy in loads(n):
            copy.start()
    barrier = pltpu.get_barrier_semaphore()
    info_own[...] = jnp.zeros(info_own.shape, f32)
    info_own[0:2, 0:tok_count] = ids_own[...].astype(f32)
    info_own[2:4, 0:tok_count] = levels_own[...].astype(f32)

    def greet(k, carry):
        pl.semaphore_signal(barrier, inc=1, device_id=(2 * lax.rem(chip + k, chips) + core, plane),
                            device_id_type=MESH)
        return carry

    lax.fori_loop(1, chips, greet, 0)
    for other in ((sibling, plane), (ep, across), (sibling, across), (ep, beside), (sibling, beside)):
        pl.semaphore_signal(barrier, inc=1, device_id=other, device_id_type=MESH)
    pl.semaphore_wait(barrier, chips + 4)

    info_swap().start()
    for n in range(2):
        for copy in swaps(n):
            copy.start()
        if n == 0:
            for m in range(3):
                home_weights(m, 0)
            away_weights(0, 0)
    for m in range(1, 3):
        away_weights(m, 0)
    for copy in loads(0):
        copy.wait()
    dispatch(0, 0)
    spread(0, 0)
    for copy in loads(1):
        copy.wait()
    dispatch(1, 0)
    spread(1, 0)
    for n in range(1, parts):
        for m in range(3):
            home_weights(m, n)
            away_weights(m, n)

    def start_relay(m, n):
        for r in range(PIECES):
            landed(piece(m, across, n, r), away_recv.at[m, n, r])
            remote(piece(m, across, n, r), piece(m, across, n, r), relay_send.at[m, n],
                   weight_recv.at[m, n, 0], 2 * chip + core, beside).start()

    def hand_over(n, group):
        return remote(alls[n].at[core, group], alls[n].at[core, group], hand_send.at[n, group],
                      hand_recv.at[n, group], sibling, plane)

    def pass_on(n, group):
        landed(alls[n].at[core, group, pl.ds(0, (chips - 1) * ROWS)], token_recv.at[n, group])
        spread_done(n, group)
        hand_over(n, group).start()

    def weights_here(m, n):
        landed(shard_strip(m, beside, n), weight_recv.at[m, n, 1])
        landed(shard_strip(m, plane, n), weight_recv.at[m, n, 2])
        landed(shard_strip(m, 3 - beside, n), weight_recv.at[m, n, 0])

    def product(left, k, group, right, cols):
        deep = min(model_width, 512)
        total = None
        for at in range(0, model_width, deep):
            term = jnp.dot(left[k, group, :, at:at + deep], right[at:at + deep, cols], preferred_element_type=f32)
            total = term if total is None else total + term
        return total

    def tiles(n):
        return pl.ds(pl.multiple_of(n * tile, tile), tile)

    def forward(n):
        cols = tiles(n)

        def step(i, carry):
            k, group = i // 2, lax.rem(i, 2)
            pre_gate = product(x_all, k, group, f_gate, cols)
            sigma = jax.nn.sigmoid(pre_gate)
            silu_val = pre_gate * sigma
            gated[k, group, :, cols] = silu_val
            slope[k, group, :, cols] = sigma * (1.0 + pre_gate * (1.0 - sigma))
            pre_up = product(x_all, k, group, f_up, cols)
            act[k, group, :, cols] = (gated[k, group, :, cols] * pre_up).astype(bf16)
            slope[k, group, :, cols] = slope[k, group, :, cols] * pre_up
            return carry

        lax.fori_loop(0, 4, step, 0)

    def backward(n):
        cols = tiles(n)

        def step(i, carry):
            k, group = i // 2, lax.rem(i, 2)
            back = product(dy_all, k, group, f_down, cols)
            d_gate[k, group, :, cols] = (back * slope[k, group, :, cols]).astype(bf16)
            d_up[k, group, :, cols] = (back * gated[k, group, :, cols]).astype(bf16)
            part = jnp.sum(act[k, group, :, cols].astype(f32) * back, axis=1, keepdims=True)
            whole = jnp.broadcast_to(part, gates_own.shape[2:])
            gates_own[k, group] = whole if n == 0 else gates_own[k, group] + whole
            return carry

        lax.fori_loop(0, 4, step, 0)

    def moved(m, i, n):
        return remote(strip(terms.at[m, i], 0, n), strip(arrived.at[m, i], 0, n), sum_send.at[m, i, n],
                      sum_recv.at[m, i, n], 2 * chip + core, beside)

    def gradients(i, n, sent):
        shard = jnp.where(i == 0, 3 - beside, jnp.where(i == 1, beside, jnp.where(i == 2, across, plane)))
        cols = pl.ds(pl.multiple_of(shard * depth, 128), depth)
        over = (((0,), (0,)), ((), ()))
        for m, left, right in ((0, x_all, d_gate), (1, x_all, d_up), (2, dy_all, act)):
            total = None
            for k in range(2):
                for group in range(2):
                    term = lax.dot_general(left[k, group, :, cols], right[k, group, :, tiles(n)], over,
                                           preferred_element_type=f32)
                    total = term if total is None else total + term
            terms[m, i, :, tiles(n)] = total.astype(bf16)
            if sent:
                moved(m, i, n).start()

    info_swap().wait()
    for copy in swaps(0):
        copy.wait_recv()
    dispatch(0, 1)
    spread(0, 1)
    pass_on(0, 0)
    for copy in swaps(1):
        copy.wait_recv()
    dispatch(1, 1)
    start_relay(0, 0)
    pass_on(0, 1)
    spread(1, 1)
    start_relay(1, 0)
    pass_on(1, 0)
    start_relay(2, 0)
    pass_on(1, 1)
    for n in range(parts):
        for m in range(2):
            weights_here(m, n)
        if n == 0:
            for group in range(2):
                landed(x_all.at[1 - core, group], hand_recv.at[0, group])
        forward(n)
        if n + 1 < parts:
            start_relay(0, n + 1)
        weights_here(2, n)
        if n == 0:
            for group in range(2):
                landed(dy_all.at[1 - core, group], hand_recv.at[1, group])
        backward(n)
        if n + 1 < parts:
            start_relay(1, n + 1)
            start_relay(2, n + 1)

        def first(i, carry, n=n):
            gradients(i, n, True)
            return carry

        lax.fori_loop(0, 2, first, 0)

    def rest(i, carry):
        gradients(2 + i // parts, lax.rem(i, parts), False)
        return carry

    lax.fori_loop(0, 2 * parts, rest, 0)

    for n in range(2):
        for group in range(2):
            hand_over(n, group).wait_send()

    def replies(k, group, other):
        wide = min(model_width, 512)

        def step(n, carry):
            cols = pl.ds(pl.multiple_of(n * wide, wide), wide)
            contract = (((1,), (1,)), ((), ()))
            total = lax.dot_general(d_gate[k, group], f_gate[cols], contract, preferred_element_type=f32)
            total = total + lax.dot_general(d_up[k, group], f_up[cols], contract, preferred_element_type=f32)
            if other is not None:
                total = total + other[group, :, cols].astype(f32)
            x_all[k, group, :, cols] = total.astype(bf16)
            return carry

        lax.fori_loop(0, model_width // wide, step, 0)

    gates_pass = remote(gates_own.at[1 - core], gates_in, pass_send.at[2], pass_recv.at[2], sibling, plane)
    gates_pass.start()

    def reply_pass(group):
        return remote(x_all.at[1 - core, group], reply_in.at[group], pass_send.at[group], pass_recv.at[group],
                      sibling, plane)

    for group in (1, 0):
        replies(1 - core, group, None)
        reply_pass(group).start()
    gates_pass.wait()
    gates_own[core] = gates_own[core] + gates_in[...]
    for group in (1, 0):
        reply_pass(group).wait()
        replies(core, group, reply_in)

        def send(k, carry, group=group):
            to = lax.rem(chip + k, chips)
            for n, (own, back) in enumerate(((x_all, reply_back), (gates_own, gates_back))):
                remote(block(own.at[core], group, to), block(back, group, chip), back_send.at[n, group],
                       back_recv.at[n, group], 2 * to + core, plane).start()
            return carry

        for n, (own, back) in enumerate(((x_all, reply_back), (gates_own, gates_back))):
            pltpu.make_async_copy(block(own.at[core], group, chip), block(back, group, chip),
                                  back_recv.at[n, group]).start()
        lax.fori_loop(1, chips, send, 0)

    def combine(group):
        landed(reply_back.at[group], back_recv.at[0, group])
        landed(gates_back.at[group], back_recv.at[1, group])
        chosen = picks(0, group)
        for j in range(chunks):
            cols = slice(j * half, (j + 1) * half)
            total = lax.dot_general(chosen, reply_back[group, :, cols], (((0,), (0,)), ((), ())),
                                    preferred_element_type=f32)
            dy_all[0, group, 0:tok_count, cols] = total.astype(bf16)
        gates_mix[group] = jnp.zeros(gates_mix.shape[1:], f32)
        for k, hit in enumerate(hits(group)):
            values = jnp.where(hit, gates_back[group, :, 0:1], 0.0)
            gates_mix[group, k:k + 1, 0:tok_count] = jnp.sum(values, axis=0, keepdims=True)

    def mixed(group):
        if group == 0:
            return []
        rows = dy_all.at[0, 1, pl.ds(0, tok_count)]
        return [remote(rows, mix_in, mix_send.at[1, 0], mix_recv.at[0], ep, across),
                remote(gates_mix.at[1], gates_mixed, mix_send.at[1, 1], mix_recv.at[1], ep, across)]

    for n in range(parts):
        if n == parts - 1:
            for group in (1, 0):
                combine(group)
                for copy in mixed(group):
                    copy.start()
        for i in range(2):
            for m in range(3):
                moved(m, i, n).wait()
                step = 128

                def add(k, carry, m=m, i=i, n=n):
                    rows = pl.ds(pl.multiple_of(k * step, step), step)
                    total = terms[m, 2 + i, rows, tiles(n)].astype(f32) + arrived[m, i, rows, tiles(n)].astype(f32)
                    terms[m, 2 + i, rows, tiles(n)] = total.astype(bf16)
                    return carry

                lax.fori_loop(0, depth // step, add, 0)
                done, out = strip(terms.at[m, 2 + i], 0, n), strip(grads[m], core, n)
                if i == 0:
                    remote(done, out, out_send.at[m, 0, n], out_recv.at[m, core, n],
                           2 * chip + parity, across).start()
                else:
                    @pl.when(core == parity)
                    def _(m=m, n=n, done=done, out=out):
                        pltpu.make_async_copy(done, out, out_recv.at[m, core, n]).start()

                    @pl.when(core != parity)
                    def _(m=m, n=n, done=done, out=out):
                        remote(done, out, out_send.at[m, 1, n], out_recv.at[m, core, n],
                               2 * chip + parity, plane).start()

    for copy in mixed(1):
        copy.wait()
    mix_own = dy_all.at[0, 0]
    for j in range(chunks):
        cols = slice(j * half, (j + 1) * half)
        total = mix_own[0:tok_count, cols].astype(f32) + mix_in[:, cols].astype(f32)
        mix_in[:, cols] = total.astype(bf16)
    for k in range(2):
        gates_mix[0, k:k + 1, 0:tok_count] = gates_mix[0, k:k + 1, 0:tok_count] + gates_mixed[k:k + 1, 0:tok_count]
    finals = [pltpu.make_async_copy(mix_in, token_out, mix_send.at[0, 0]),
              pltpu.make_async_copy(gates_mix.at[0], gates_out, mix_send.at[0, 1])]
    for copy in finals:
        copy.start()

    for n in range(parts):
        for m in range(3):
            landed(shard_strip(m, across, n), relay_send.at[m, n])
            for part in range(2):
                landed(strip(weights[m], part, n), weight_send.at[m, n, part])

            @pl.when(jnp.logical_not(away))
            def _(m=m, n=n):
                landed(strip(weights[m], 0, n), weight_send.at[m, n, 2])
            landed(strip(terms.at[m, 2], 0, n), out_send.at[m, 0, n])

            @pl.when(core != parity)
            def _(m=m, n=n):
                landed(strip(terms.at[m, 3], 0, n), out_send.at[m, 1, n])
            for part in range(2):
                landed(strip(grads[m], part, n), out_recv.at[m, part, n])
    for n in range(2):
        for copy in swaps(n):
            copy.wait_send()
    for n, own in enumerate((x_all, gates_own)):
        for group in range(2):
            landed(own.at[core, group, pl.ds(0, (chips - 1) * ROWS)], back_send.at[n, group])
    for copy in finals:
        copy.wait()


def shards(tokens, upstream, expert_ids, gate_values, w_gate, w_up, w_down):
    experts = lax.axis_size("ep")
    chips = experts // 2
    tok_count, top_count = expert_ids.shape
    model_width = tokens.shape[1]
    depth, width = w_gate.shape[1:]
    half = width // 2
    bf16 = jnp.bfloat16
    lanes = -(-tok_count // 128) * 128
    anywhere = pl.BlockSpec(memory_space=pl.ANY)
    dma = pltpu.SemaphoreType.DMA
    tall = chips * ROWS
    rows_buffer = pltpu.VMEM((2, 2, tall, model_width), bf16)
    full_buffer = pltpu.VMEM((4 * depth, half), bf16)
    wide_buffer = pltpu.VMEM((2, 2, tall, half), jnp.float32)
    narrow_buffer = pltpu.VMEM((2, 2, tall, half), bf16)
    grad_shape = jax.ShapeDtypeStruct((3, depth, width), bf16)
    mix_shape = jax.ShapeDtypeStruct((tok_count, model_width), bf16)
    info_shape = jax.ShapeDtypeStruct((8, lanes), jnp.float32)
    parts = max(1, half // 256)
    token_grad, gate_grad, grads = pl.pallas_call(
        functools.partial(layer_kernel, chips),
        out_shape=[mix_shape, info_shape, grad_shape],
        in_specs=[anywhere] * 2 + [pl.BlockSpec(memory_space=pltpu.VMEM)] * 2 + [anywhere] * 3,
        out_specs=[anywhere] * 3,
        scratch_shapes=[
            rows_buffer, rows_buffer, full_buffer, full_buffer, full_buffer,
            wide_buffer, wide_buffer, narrow_buffer, narrow_buffer, narrow_buffer,
            pltpu.VMEM((3, 4, depth, half), bf16), pltpu.VMEM((3, 2, depth, half), bf16),
            pltpu.VMEM((2, tall, model_width), bf16), pltpu.VMEM((2, tall, model_width), bf16),
            pltpu.VMEM((2, 2, tall, 128), jnp.float32), pltpu.VMEM((2, tall, 128), jnp.float32),
            pltpu.VMEM((2, tall, 128), jnp.float32), pltpu.VMEM((2, 8, lanes), jnp.float32),
            pltpu.VMEM((8, lanes), jnp.float32), pltpu.VMEM((8, lanes), jnp.float32), pltpu.VMEM((tok_count, model_width), bf16),
            pltpu.VMEM((8, lanes), jnp.float32),
            dma((2, model_width // half)), dma((2, model_width // half)), dma((2, model_width // half)),
            dma((2,)), dma((2, 2)),
            dma((2, 2)), dma((2, 2)), dma((2, 2)), dma((2, 2)),
            dma((3, parts, 3)), dma((3, parts, 3)), dma((3, parts, PIECES)), dma((3, parts)),
            dma((3, 2, parts)), dma((3, 2, parts)), dma((3,)), dma((3,)), dma((3, 2, parts)), dma((3, 2, parts)),
            dma((2, 2)), dma((2, 2)),
            dma((2, 2)), dma((2,))],
        compiler_params=pltpu.CompilerParams(has_side_effects=True, collective_id=0, vmem_limit_bytes=60 << 20),
        name="expert_layer",
    )(tokens, upstream, expert_ids.T, gate_values.T, w_gate[0], w_up[0], w_down[0])

    gate_grad = gate_grad[:top_count, :tok_count].T
    gate_grad = (gate_grad / gate_values.astype(jnp.float32)).astype(bf16)
    return token_grad, gate_grad, grads[0:1], grads[1:2], grads[2:3]


def solution(mesh):
    tokens_spec, weights_spec = P(("ep", "edp"), None), P("ep", "edp", None)
    return jax.shard_map(
        shards, mesh=mesh,
        in_specs=(tokens_spec,) * 4 + (weights_spec,) * 3,
        out_specs=(tokens_spec,) * 2 + (weights_spec,) * 3,
        check_vma=False,
    )
```

```python
import functools

import jax
import jax.numpy as jnp
from jax import lax
from jax.experimental import pallas as pl
from jax.experimental.pallas import tpu as pltpu
from jax.sharding import PartitionSpec as P

MESH = pl.DeviceIdType.MESH
ROWS = 16
PIECES = 1


def place():
    ep, plane = lax.axis_index("ep"), lax.axis_index("edp")
    core = lax.rem(ep, 2)
    parity = plane // 2
    beside = plane + 1 - 2 * lax.rem(plane, 2)
    across = 3 - plane
    return ep, ep // 2, core, plane, parity, beside, across


def remote(src, dst, send, recv, ep, plane):
    return pltpu.make_async_remote_copy(
        src_ref=src, dst_ref=dst, send_sem=send, recv_sem=recv,
        device_id=(ep, plane), device_id_type=MESH,
    )


def landed(ref, sem):
    pltpu.make_async_copy(ref, ref, sem).wait()


def layer_kernel(chips, tokens, upstream, ids_own, levels_own, w_gate, w_up, w_down,
                 token_out, gates_out, g_all,
                 x_all, dy_all, f_gate, f_up, f_down, slope, gated, act, d_gate, d_up, terms, arrived,
                 x_stage, dy_stage, gates_own, gates_in, gates_back, gates_mix, info_own, info_in,
                 mix_in, gates_mixed,
                 load_sem, swap_send, swap_recv, info_sem, stay_sem,
                 token_send, token_recv, hand_send, hand_recv, weight_send, weight_recv, away_recv, relay_send,
                 sum_send, sum_recv, pass_send, pass_recv, out_send, out_recv, back_send, back_recv,
                 mix_send, mix_recv):
    ep, chip, core, plane, parity, beside, across = place()
    depth, width = w_gate.shape
    half = width // 2
    tile = min(half, 256)
    parts = half // tile
    tok_count, model_width = tokens.shape
    tall = chips * ROWS
    sibling = ep + 1 - 2 * core
    away = core != parity
    weights = (w_gate, w_up, w_down)
    fulls = (f_gate, f_up, f_down)
    grads = [g_all.at[m] for m in range(3)]
    stages, alls = (x_stage, dy_stage), (x_all, dy_all)
    reply_back, reply_in = x_stage, dy_stage
    f32, bf16 = jnp.float32, jnp.bfloat16

    def rows_of(ref, shard):
        return ref.at[pl.ds(pl.multiple_of(shard * depth, 16), depth)]

    def columns(ref, part):
        return ref.at[:, pl.ds(pl.multiple_of(part * half, 128), half)]

    def strip(ref, part, n):
        return ref.at[:, pl.ds(pl.multiple_of(part * half + n * tile, 128), tile)]

    def shard_strip(m, shard, n):
        return strip(rows_of(fulls[m], shard), 0, n)

    def block(ref, group, index):
        return ref.at[group, pl.ds(pl.multiple_of(index * ROWS, ROWS), ROWS)]

    chunks = model_width // half
    fit = depth // tok_count
    slabs = -(-chunks // fit)

    def chunk_of(n, group, j):
        slab = slabs * (2 * n + group) + j // fit
        return terms.at[slab // 4, slab % 4, pl.ds(j % fit * tok_count, tok_count)]

    def source_of(n, j):
        return (tokens, upstream)[n].at[:, pl.ds(j * half, half)]

    def loads(n):
        return [pltpu.make_async_copy(source_of(n, j), chunk_of(n, 0, j), load_sem.at[n, j]) for j in range(chunks)]

    def swaps(n):
        return [remote(source_of(n, j), chunk_of(n, 1, j), swap_send.at[n, j], swap_recv.at[n, j], ep, across)
                for j in range(chunks)]

    def info_swap():
        return remote(info_own, info_in, info_sem.at[0], info_sem.at[1], ep, across)

    def hits(group):
        info = info_own if group == 0 else info_in
        ids = [info[k:k + 1, :tok_count] for k in range(2)]
        names = lax.broadcasted_iota(jnp.int32, (2 * chips, tok_count), 0).astype(f32)
        named = [names == one for one in ids]
        ones = [jnp.where(one, 1.0, 0.0) for one in named]
        earlier = (lax.broadcasted_iota(jnp.int32, (tok_count, tok_count), 0)
                   < lax.broadcasted_iota(jnp.int32, (tok_count, tok_count), 1))
        ranks = jnp.dot((ones[0] + ones[1]).astype(bf16), jnp.where(earlier, 1.0, 0.0).astype(bf16),
                        preferred_element_type=f32)
        rows = lax.broadcasted_iota(jnp.int32, (tall, tok_count), 0)
        slot = (rows + (rows // ROWS + parity) * ROWS).astype(f32)
        return [slot == ids[k] * ROWS + jnp.sum(ones[k] * ranks, axis=0, keepdims=True) for k in range(2)]

    def picks(n, group):
        info = info_own if group == 0 else info_in
        levels = [info[2 + k:3 + k, :tok_count] if n else jnp.ones((1, tok_count), f32) for k in range(2)]
        terms_of = [jnp.where(hit, level, 0.0) for hit, level in zip(hits(group), levels)]
        return (terms_of[0] + terms_of[1]).astype(bf16)

    def dispatch(n, group):
        chosen = picks(n, group)
        for j in range(chunks):
            rows = jnp.dot(chosen, chunk_of(n, group, j)[...], preferred_element_type=f32)
            stages[n][group, :, j * half:(j + 1) * half] = rows.astype(bf16)

    def stays(n, group):
        return pltpu.make_async_copy(block(stages[n], group, chip), block(alls[n].at[core], group, chip),
                                     stay_sem.at[n, group])

    def spread(n, group):
        def send(k, carry):
            to = lax.rem(chip + k, chips)
            remote(block(stages[n], group, to), block(alls[n].at[core], group, chip), token_send.at[n, group],
                   token_recv.at[n, group], 2 * to + core, plane).start()
            return carry

        stays(n, group).start()
        lax.fori_loop(1, chips, send, 0)

    def spread_done(n, group):
        stays(n, group).wait()
        landed(stages[n].at[group, pl.ds(0, (chips - 1) * ROWS)], token_send.at[n, group])

    size = depth // PIECES

    def piece(m, shard, n, r):
        return strip(fulls[m].at[pl.ds(pl.multiple_of(shard * depth + r * size, 16), size)], 0, n)

    def away_weights(m, n):
        @pl.when(away)
        def _():
            for part in range(2):
                for r in range(PIECES):
                    remote(strip(weights[m].at[pl.ds(r * size, size)], part, n), piece(m, plane, n, r),
                           weight_send.at[m, n, part], away_recv.at[m, n, r], 2 * chip + part, across).start()

    def home_weights(m, n):
        @pl.when(jnp.logical_not(away))
        def _():
            for part in range(2):
                remote(strip(weights[m], part, n), shard_strip(m, plane, n), weight_send.at[m, n, part],
                       weight_recv.at[m, n, 1], 2 * chip + part, beside).start()
            pltpu.make_async_copy(strip(weights[m], core, n), shard_strip(m, plane, n),
                                  weight_recv.at[m, n, 2]).start()
            remote(strip(weights[m], 1 - core, n), shard_strip(m, plane, n), weight_send.at[m, n, 2],
                   weight_recv.at[m, n, 2], sibling, plane).start()

    for n in range(2):
        for copy in loads(n):
            copy.start()
    barrier = pltpu.get_barrier_semaphore()
    info_own[...] = jnp.zeros(info_own.shape, f32)
    info_own[0:2, 0:tok_count] = ids_own[...].astype(f32)
    info_own[2:4, 0:tok_count] = levels_own[...].astype(f32)

    def greet(k, carry):
        pl.semaphore_signal(barrier, inc=1, device_id=(2 * lax.rem(chip + k, chips) + core, plane),
                            device_id_type=MESH)
        return carry

    lax.fori_loop(1, chips, greet, 0)
    for other in ((sibling, plane), (ep, across), (sibling, across), (ep, beside), (sibling, beside)):
        pl.semaphore_signal(barrier, inc=1, device_id=other, device_id_type=MESH)
    pl.semaphore_wait(barrier, chips + 4)

    info_swap().start()
    for n in range(2):
        for copy in swaps(n):
            copy.start()
    for copy in loads(0):
        copy.wait()
    dispatch(0, 0)
    spread(0, 0)
    for copy in loads(1):
        copy.wait()
    dispatch(1, 0)
    spread(1, 0)
    for m in range(3):
        home_weights(m, 0)
        away_weights(m, 0)
    for n in range(1, parts):
        for m in range(3):
            home_weights(m, n)
            away_weights(m, n)

    def start_relay(m, n):
        for r in range(PIECES):
            landed(piece(m, across, n, r), away_recv.at[m, n, r])
            remote(piece(m, across, n, r), piece(m, across, n, r), relay_send.at[m, n],
                   weight_recv.at[m, n, 0], 2 * chip + core, beside).start()

    def hand_over(n, group):
        return remote(alls[n].at[core, group], alls[n].at[core, group], hand_send.at[n, group],
                      hand_recv.at[n, group], sibling, plane)

    def pass_on(n, group):
        landed(alls[n].at[core, group, pl.ds(0, (chips - 1) * ROWS)], token_recv.at[n, group])
        spread_done(n, group)
        hand_over(n, group).start()

    def weights_here(m, n):
        landed(shard_strip(m, beside, n), weight_recv.at[m, n, 1])
        landed(shard_strip(m, plane, n), weight_recv.at[m, n, 2])
        landed(shard_strip(m, 3 - beside, n), weight_recv.at[m, n, 0])

    def product(left, k, group, right, cols):
        deep = min(model_width, 512)
        total = None
        for at in range(0, model_width, deep):
            term = jnp.dot(left[k, group, :, at:at + deep], right[at:at + deep, cols], preferred_element_type=f32)
            total = term if total is None else total + term
        return total

    def tiles(n):
        return pl.ds(pl.multiple_of(n * tile, tile), tile)

    def forward(n):
        cols = tiles(n)

        def step(i, carry):
            k, group = i // 2, lax.rem(i, 2)
            pre_gate = product(x_all, k, group, f_gate, cols)
            sigma = jax.nn.sigmoid(pre_gate)
            silu_val = pre_gate * sigma
            gated[k, group, :, cols] = silu_val
            slope[k, group, :, cols] = sigma * (1.0 + pre_gate * (1.0 - sigma))
            pre_up = product(x_all, k, group, f_up, cols)
            act[k, group, :, cols] = (gated[k, group, :, cols] * pre_up).astype(bf16)
            slope[k, group, :, cols] = slope[k, group, :, cols] * pre_up
            return carry

        lax.fori_loop(0, 4, step, 0)

    def backward(n):
        cols = tiles(n)

        def step(i, carry):
            k, group = i // 2, lax.rem(i, 2)
            back = product(dy_all, k, group, f_down, cols)
            d_gate[k, group, :, cols] = (back * slope[k, group, :, cols]).astype(bf16)
            d_up[k, group, :, cols] = (back * gated[k, group, :, cols]).astype(bf16)
            part = jnp.sum(act[k, group, :, cols].astype(f32) * back, axis=1, keepdims=True)
            whole = jnp.broadcast_to(part, gates_own.shape[2:])
            gates_own[k, group] = whole if n == 0 else gates_own[k, group] + whole
            return carry

        lax.fori_loop(0, 4, step, 0)

    def moved(m, i, n):
        return remote(strip(terms.at[m, i], 0, n), strip(arrived.at[m, i], 0, n), sum_send.at[m, i, n],
                      sum_recv.at[m, i, n], 2 * chip + core, beside)

    def gradients(i, n, sent):
        shard = jnp.where(i == 0, 3 - beside, jnp.where(i == 1, beside, jnp.where(i == 2, across, plane)))
        cols = pl.ds(pl.multiple_of(shard * depth, 128), depth)
        over = (((0,), (0,)), ((), ()))
        for m, left, right in ((0, x_all, d_gate), (1, x_all, d_up), (2, dy_all, act)):
            total = None
            for k in range(2):
                for group in range(2):
                    term = lax.dot_general(left[k, group, :, cols], right[k, group, :, tiles(n)], over,
                                           preferred_element_type=f32)
                    total = term if total is None else total + term
            terms[m, i, :, tiles(n)] = total.astype(bf16)
            if sent:
                moved(m, i, n).start()

    info_swap().wait()
    for copy in swaps(0):
        copy.wait_recv()
    dispatch(0, 1)
    spread(0, 1)
    pass_on(0, 0)
    for copy in swaps(1):
        copy.wait_recv()
    dispatch(1, 1)
    start_relay(0, 0)
    pass_on(0, 1)
    spread(1, 1)
    start_relay(1, 0)
    pass_on(1, 0)
    start_relay(2, 0)
    pass_on(1, 1)
    for n in range(parts):
        for m in range(2):
            weights_here(m, n)
        if n == 0:
            for group in range(2):
                landed(x_all.at[1 - core, group], hand_recv.at[0, group])
        forward(n)
        if n + 1 < parts:
            start_relay(0, n + 1)
        weights_here(2, n)
        if n == 0:
            for group in range(2):
                landed(dy_all.at[1 - core, group], hand_recv.at[1, group])
        backward(n)
        if n + 1 < parts:
            start_relay(1, n + 1)
            start_relay(2, n + 1)

        def first(i, carry, n=n):
            gradients(i, n, True)
            return carry

        lax.fori_loop(0, 2, first, 0)

    def rest(i, carry):
        gradients(2 + i // parts, lax.rem(i, parts), False)
        return carry

    lax.fori_loop(0, 2 * parts, rest, 0)

    for n in range(2):
        for group in range(2):
            hand_over(n, group).wait_send()

    def replies(k, group, other):
        wide = min(model_width, 512)

        def step(n, carry):
            cols = pl.ds(pl.multiple_of(n * wide, wide), wide)
            contract = (((1,), (1,)), ((), ()))
            total = lax.dot_general(d_gate[k, group], f_gate[cols], contract, preferred_element_type=f32)
            total = total + lax.dot_general(d_up[k, group], f_up[cols], contract, preferred_element_type=f32)
            if other is not None:
                total = total + other[group, :, cols].astype(f32)
            x_all[k, group, :, cols] = total.astype(bf16)
            return carry

        lax.fori_loop(0, model_width // wide, step, 0)

    gates_pass = remote(gates_own.at[1 - core], gates_in, pass_send.at[2], pass_recv.at[2], sibling, plane)
    gates_pass.start()

    def reply_pass(group):
        return remote(x_all.at[1 - core, group], reply_in.at[group], pass_send.at[group], pass_recv.at[group],
                      sibling, plane)

    for group in (1, 0):
        replies(1 - core, group, None)
        reply_pass(group).start()
    gates_pass.wait()
    gates_own[core] = gates_own[core] + gates_in[...]
    for group in (1, 0):
        reply_pass(group).wait()
        replies(core, group, reply_in)

        def send(k, carry, group=group):
            to = lax.rem(chip + k, chips)
            for n, (own, back) in enumerate(((x_all, reply_back), (gates_own, gates_back))):
                remote(block(own.at[core], group, to), block(back, group, chip), back_send.at[n, group],
                       back_recv.at[n, group], 2 * to + core, plane).start()
            return carry

        for n, (own, back) in enumerate(((x_all, reply_back), (gates_own, gates_back))):
            pltpu.make_async_copy(block(own.at[core], group, chip), block(back, group, chip),
                                  back_recv.at[n, group]).start()
        lax.fori_loop(1, chips, send, 0)

    def combine(group):
        landed(reply_back.at[group], back_recv.at[0, group])
        landed(gates_back.at[group], back_recv.at[1, group])
        chosen = picks(0, group)
        for j in range(chunks):
            cols = slice(j * half, (j + 1) * half)
            total = lax.dot_general(chosen, reply_back[group, :, cols], (((0,), (0,)), ((), ())),
                                    preferred_element_type=f32)
            dy_all[0, group, 0:tok_count, cols] = total.astype(bf16)
        gates_mix[group] = jnp.zeros(gates_mix.shape[1:], f32)
        for k, hit in enumerate(hits(group)):
            values = jnp.where(hit, gates_back[group, :, 0:1], 0.0)
            gates_mix[group, k:k + 1, 0:tok_count] = jnp.sum(values, axis=0, keepdims=True)

    def mixed(group):
        if group == 0:
            return []
        rows = dy_all.at[0, 1, pl.ds(0, tok_count)]
        return [remote(rows, mix_in, mix_send.at[1, 0], mix_recv.at[0], ep, across),
                remote(gates_mix.at[1], gates_mixed, mix_send.at[1, 1], mix_recv.at[1], ep, across)]

    for n in range(parts):
        if n == parts - 1:
            for group in (1, 0):
                combine(group)
                for copy in mixed(group):
                    copy.start()
        for i in range(2):
            if i == 1 and n == parts - 1:
                for copy in mixed(1):
                    copy.wait()
                mix_own = dy_all.at[0, 0]
                for j in range(chunks):
                    cols = slice(j * half, (j + 1) * half)
                    total = mix_own[0:tok_count, cols].astype(f32) + mix_in[:, cols].astype(f32)
                    mix_in[:, cols] = total.astype(bf16)
                for k in range(2):
                    gates_mix[0, k:k + 1, 0:tok_count] = gates_mix[0, k:k + 1, 0:tok_count] + gates_mixed[k:k + 1, 0:tok_count]
                finals = [pltpu.make_async_copy(mix_in, token_out, mix_send.at[0, 0]),
                          pltpu.make_async_copy(gates_mix.at[0], gates_out, mix_send.at[0, 1])]
                for copy in finals:
                    copy.start()
            for m in range(3):
                moved(m, i, n).wait()
                step = 128

                def add(k, carry, m=m, i=i, n=n):
                    rows = pl.ds(pl.multiple_of(k * step, step), step)
                    total = terms[m, 2 + i, rows, tiles(n)].astype(f32) + arrived[m, i, rows, tiles(n)].astype(f32)
                    terms[m, 2 + i, rows, tiles(n)] = total.astype(bf16)
                    return carry

                lax.fori_loop(0, depth // step, add, 0)
                done, out = strip(terms.at[m, 2 + i], 0, n), strip(grads[m], core, n)
                if i == 0:
                    remote(done, out, out_send.at[m, 0, n], out_recv.at[m, core, n],
                           2 * chip + parity, across).start()
                else:
                    @pl.when(core == parity)
                    def _(m=m, n=n, done=done, out=out):
                        pltpu.make_async_copy(done, out, out_recv.at[m, core, n]).start()

                    @pl.when(core != parity)
                    def _(m=m, n=n, done=done, out=out):
                        remote(done, out, out_send.at[m, 1, n], out_recv.at[m, core, n],
                               2 * chip + parity, plane).start()

    for n in range(parts):
        for m in range(3):
            landed(shard_strip(m, across, n), relay_send.at[m, n])
            for part in range(2):
                landed(strip(weights[m], part, n), weight_send.at[m, n, part])

            @pl.when(jnp.logical_not(away))
            def _(m=m, n=n):
                landed(strip(weights[m], 0, n), weight_send.at[m, n, 2])
            landed(strip(terms.at[m, 2], 0, n), out_send.at[m, 0, n])

            @pl.when(core != parity)
            def _(m=m, n=n):
                landed(strip(terms.at[m, 3], 0, n), out_send.at[m, 1, n])
            for part in range(2):
                landed(strip(grads[m], part, n), out_recv.at[m, part, n])
    for n in range(2):
        for copy in swaps(n):
            copy.wait_send()
    for n, own in enumerate((x_all, gates_own)):
        for group in range(2):
            landed(own.at[core, group, pl.ds(0, (chips - 1) * ROWS)], back_send.at[n, group])
    for copy in finals:
        copy.wait()


def shards(tokens, upstream, expert_ids, gate_values, w_gate, w_up, w_down):
    experts = lax.axis_size("ep")
    chips = experts // 2
    tok_count, top_count = expert_ids.shape
    model_width = tokens.shape[1]
    depth, width = w_gate.shape[1:]
    half = width // 2
    bf16 = jnp.bfloat16
    lanes = -(-tok_count // 128) * 128
    anywhere = pl.BlockSpec(memory_space=pl.ANY)
    dma = pltpu.SemaphoreType.DMA
    tall = chips * ROWS
    rows_buffer = pltpu.VMEM((2, 2, tall, model_width), bf16)
    full_buffer = pltpu.VMEM((4 * depth, half), bf16)
    wide_buffer = pltpu.VMEM((2, 2, tall, half), jnp.float32)
    narrow_buffer = pltpu.VMEM((2, 2, tall, half), bf16)
    grad_shape = jax.ShapeDtypeStruct((3, depth, width), bf16)
    mix_shape = jax.ShapeDtypeStruct((tok_count, model_width), bf16)
    info_shape = jax.ShapeDtypeStruct((8, lanes), jnp.float32)
    parts = max(1, half // 256)
    token_grad, gate_grad, grads = pl.pallas_call(
        functools.partial(layer_kernel, chips),
        out_shape=[mix_shape, info_shape, grad_shape],
        in_specs=[anywhere] * 2 + [pl.BlockSpec(memory_space=pltpu.VMEM)] * 2 + [anywhere] * 3,
        out_specs=[anywhere] * 3,
        scratch_shapes=[
            rows_buffer, rows_buffer, full_buffer, full_buffer, full_buffer,
            wide_buffer, wide_buffer, narrow_buffer, narrow_buffer, narrow_buffer,
            pltpu.VMEM((3, 4, depth, half), bf16), pltpu.VMEM((3, 2, depth, half), bf16),
            pltpu.VMEM((2, tall, model_width), bf16), pltpu.VMEM((2, tall, model_width), bf16),
            pltpu.VMEM((2, 2, tall, 128), jnp.float32), pltpu.VMEM((2, tall, 128), jnp.float32),
            pltpu.VMEM((2, tall, 128), jnp.float32), pltpu.VMEM((2, 8, lanes), jnp.float32),
            pltpu.VMEM((8, lanes), jnp.float32), pltpu.VMEM((8, lanes), jnp.float32), pltpu.VMEM((tok_count, model_width), bf16),
            pltpu.VMEM((8, lanes), jnp.float32),
            dma((2, model_width // half)), dma((2, model_width // half)), dma((2, model_width // half)),
            dma((2,)), dma((2, 2)),
            dma((2, 2)), dma((2, 2)), dma((2, 2)), dma((2, 2)),
            dma((3, parts, 3)), dma((3, parts, 3)), dma((3, parts, PIECES)), dma((3, parts)),
            dma((3, 2, parts)), dma((3, 2, parts)), dma((3,)), dma((3,)), dma((3, 2, parts)), dma((3, 2, parts)),
            dma((2, 2)), dma((2, 2)),
            dma((2, 2)), dma((2,))],
        compiler_params=pltpu.CompilerParams(has_side_effects=True, collective_id=0, vmem_limit_bytes=60 << 20),
        name="expert_layer",
    )(tokens, upstream, expert_ids.T, gate_values.T, w_gate[0], w_up[0], w_down[0])

    gate_grad = gate_grad[:top_count, :tok_count].T
    gate_grad = (gate_grad / gate_values.astype(jnp.float32)).astype(bf16)
    return token_grad, gate_grad, grads[0:1], grads[1:2], grads[2:3]


def solution(mesh):
    tokens_spec, weights_spec = P(("ep", "edp"), None), P("ep", "edp", None)
    return jax.shard_map(
        shards, mesh=mesh,
        in_specs=(tokens_spec,) * 4 + (weights_spec,) * 3,
        out_specs=(tokens_spec,) * 2 + (weights_spec,) * 3,
        check_vma=False,
    )
```

```python
import functools

import jax
import jax.numpy as jnp
from jax import lax
from jax.experimental import pallas as pl
from jax.experimental.pallas import tpu as pltpu
from jax.sharding import PartitionSpec as P

MESH = pl.DeviceIdType.MESH
ROWS = 16
PIECES = 1


def place():
    ep, plane = lax.axis_index("ep"), lax.axis_index("edp")
    core = lax.rem(ep, 2)
    parity = plane // 2
    beside = plane + 1 - 2 * lax.rem(plane, 2)
    across = 3 - plane
    return ep, ep // 2, core, plane, parity, beside, across


def remote(src, dst, send, recv, ep, plane):
    return pltpu.make_async_remote_copy(
        src_ref=src, dst_ref=dst, send_sem=send, recv_sem=recv,
        device_id=(ep, plane), device_id_type=MESH,
    )


def landed(ref, sem):
    pltpu.make_async_copy(ref, ref, sem).wait()


def layer_kernel(chips, tokens, upstream, ids_own, levels_own, w_gate, w_up, w_down,
                 token_out, gates_out, g_all,
                 x_all, dy_all, f_gate, f_up, f_down, slope, gated, act, d_gate, d_up, terms, arrived,
                 x_stage, dy_stage, gates_own, gates_in, gates_back, gates_mix, info_own, info_in,
                 mix_in, gates_mixed,
                 load_sem, swap_send, swap_recv, info_sem, stay_sem,
                 token_send, token_recv, hand_send, hand_recv, weight_send, weight_recv, away_recv, relay_send,
                 sum_send, sum_recv, pass_send, pass_recv, out_send, out_recv, back_send, back_recv,
                 mix_send, mix_recv):
    ep, chip, core, plane, parity, beside, across = place()
    depth, width = w_gate.shape
    half = width // 2
    tile = min(half, 256)
    parts = half // tile
    tok_count, model_width = tokens.shape
    tall = chips * ROWS
    sibling = ep + 1 - 2 * core
    away = core != parity
    weights = (w_gate, w_up, w_down)
    fulls = (f_gate, f_up, f_down)
    grads = [g_all.at[m] for m in range(3)]
    stages, alls = (x_stage, dy_stage), (x_all, dy_all)
    reply_back, reply_in = x_stage, dy_stage
    f32, bf16 = jnp.float32, jnp.bfloat16

    def rows_of(ref, shard):
        return ref.at[pl.ds(pl.multiple_of(shard * depth, 16), depth)]

    def columns(ref, part):
        return ref.at[:, pl.ds(pl.multiple_of(part * half, 128), half)]

    def strip(ref, part, n):
        return ref.at[:, pl.ds(pl.multiple_of(part * half + n * tile, 128), tile)]

    def shard_strip(m, shard, n):
        return strip(rows_of(fulls[m], shard), 0, n)

    def block(ref, group, index):
        return ref.at[group, pl.ds(pl.multiple_of(index * ROWS, ROWS), ROWS)]

    chunks = model_width // half
    fit = depth // tok_count
    slabs = -(-chunks // fit)

    def chunk_of(n, group, j):
        slab = slabs * (2 * n + group) + j // fit
        return terms.at[slab // 4, slab % 4, pl.ds(j % fit * tok_count, tok_count)]

    def source_of(n, j):
        return (tokens, upstream)[n].at[:, pl.ds(j * half, half)]

    def loads(n):
        return [pltpu.make_async_copy(source_of(n, j), chunk_of(n, 0, j), load_sem.at[n, j]) for j in range(chunks)]

    def swaps(n):
        return [remote(source_of(n, j), chunk_of(n, 1, j), swap_send.at[n, j], swap_recv.at[n, j], ep, across)
                for j in range(chunks)]

    def info_swap():
        return remote(info_own, info_in, info_sem.at[0], info_sem.at[1], ep, across)

    def hits(group):
        info = info_own if group == 0 else info_in
        ids = [info[k:k + 1, :tok_count] for k in range(2)]
        names = lax.broadcasted_iota(jnp.int32, (2 * chips, tok_count), 0).astype(f32)
        named = [names == one for one in ids]
        ones = [jnp.where(one, 1.0, 0.0) for one in named]
        earlier = (lax.broadcasted_iota(jnp.int32, (tok_count, tok_count), 0)
                   < lax.broadcasted_iota(jnp.int32, (tok_count, tok_count), 1))
        ranks = jnp.dot((ones[0] + ones[1]).astype(bf16), jnp.where(earlier, 1.0, 0.0).astype(bf16),
                        preferred_element_type=f32)
        rows = lax.broadcasted_iota(jnp.int32, (tall, tok_count), 0)
        slot = (rows + (rows // ROWS + parity) * ROWS).astype(f32)
        return [slot == ids[k] * ROWS + jnp.sum(ones[k] * ranks, axis=0, keepdims=True) for k in range(2)]

    def picks(n, group):
        info = info_own if group == 0 else info_in
        levels = [info[2 + k:3 + k, :tok_count] if n else jnp.ones((1, tok_count), f32) for k in range(2)]
        terms_of = [jnp.where(hit, level, 0.0) for hit, level in zip(hits(group), levels)]
        return (terms_of[0] + terms_of[1]).astype(bf16)

    def dispatch(n, group):
        chosen = picks(n, group)
        for j in range(chunks):
            rows = jnp.dot(chosen, chunk_of(n, group, j)[...], preferred_element_type=f32)
            stages[n][group, :, j * half:(j + 1) * half] = rows.astype(bf16)

    def stays(n, group):
        return pltpu.make_async_copy(block(stages[n], group, chip), block(alls[n].at[core], group, chip),
                                     stay_sem.at[n, group])

    def spread(n, group):
        def send(k, carry):
            to = lax.rem(chip + k, chips)
            remote(block(stages[n], group, to), block(alls[n].at[core], group, chip), token_send.at[n, group],
                   token_recv.at[n, group], 2 * to + core, plane).start()
            return carry

        stays(n, group).start()
        lax.fori_loop(1, chips, send, 0)

    def spread_done(n, group):
        stays(n, group).wait()
        landed(stages[n].at[group, pl.ds(0, (chips - 1) * ROWS)], token_send.at[n, group])

    size = depth // PIECES

    def piece(m, shard, n, r):
        return strip(fulls[m].at[pl.ds(pl.multiple_of(shard * depth + r * size, 16), size)], 0, n)

    def away_weights(m, n):
        @pl.when(away)
        def _():
            for part in range(2):
                for r in range(PIECES):
                    remote(strip(weights[m].at[pl.ds(r * size, size)], part, n), piece(m, plane, n, r),
                           weight_send.at[m, n, part], away_recv.at[m, n, r], 2 * chip + part, across).start()

    def home_weights(m, n):
        @pl.when(jnp.logical_not(away))
        def _():
            for part in range(2):
                remote(strip(weights[m], part, n), shard_strip(m, plane, n), weight_send.at[m, n, part],
                       weight_recv.at[m, n, 1], 2 * chip + part, beside).start()
            pltpu.make_async_copy(strip(weights[m], core, n), shard_strip(m, plane, n),
                                  weight_recv.at[m, n, 2]).start()
            remote(strip(weights[m], 1 - core, n), shard_strip(m, plane, n), weight_send.at[m, n, 2],
                   weight_recv.at[m, n, 2], sibling, plane).start()

    barrier = pltpu.get_barrier_semaphore()

    def greet(k, carry):
        pl.semaphore_signal(barrier, inc=1, device_id=(2 * lax.rem(chip + k, chips) + core, plane),
                            device_id_type=MESH)
        return carry

    lax.fori_loop(1, chips, greet, 0)
    for other in ((sibling, plane), (ep, across), (sibling, across), (ep, beside), (sibling, beside)):
        pl.semaphore_signal(barrier, inc=1, device_id=other, device_id_type=MESH)
    for n in range(2):
        for copy in loads(n):
            copy.start()
    info_own[...] = jnp.zeros(info_own.shape, f32)
    info_own[0:2, 0:tok_count] = ids_own[...].astype(f32)
    info_own[2:4, 0:tok_count] = levels_own[...].astype(f32)

    pl.semaphore_wait(barrier, chips + 4)

    info_swap().start()
    for n in range(2):
        for copy in swaps(n):
            copy.start()
    for copy in loads(0):
        copy.wait()
    dispatch(0, 0)
    spread(0, 0)
    for copy in loads(1):
        copy.wait()
    dispatch(1, 0)
    spread(1, 0)
    for m in range(3):
        home_weights(m, 0)
        away_weights(m, 0)
    for n in range(1, parts):
        for m in range(3):
            home_weights(m, n)
            away_weights(m, n)

    def start_relay(m, n):
        for r in range(PIECES):
            landed(piece(m, across, n, r), away_recv.at[m, n, r])
            remote(piece(m, across, n, r), piece(m, across, n, r), relay_send.at[m, n],
                   weight_recv.at[m, n, 0], 2 * chip + core, beside).start()

    def hand_over(n, group):
        return remote(alls[n].at[core, group], alls[n].at[core, group], hand_send.at[n, group],
                      hand_recv.at[n, group], sibling, plane)

    def pass_on(n, group):
        landed(alls[n].at[core, group, pl.ds(0, (chips - 1) * ROWS)], token_recv.at[n, group])
        spread_done(n, group)
        hand_over(n, group).start()

    def weights_here(m, n):
        landed(shard_strip(m, beside, n), weight_recv.at[m, n, 1])
        landed(shard_strip(m, plane, n), weight_recv.at[m, n, 2])
        landed(shard_strip(m, 3 - beside, n), weight_recv.at[m, n, 0])

    def product(left, k, group, right, cols):
        deep = min(model_width, 512)
        total = None
        for at in range(0, model_width, deep):
            term = jnp.dot(left[k, group, :, at:at + deep], right[at:at + deep, cols], preferred_element_type=f32)
            total = term if total is None else total + term
        return total

    def tiles(n):
        return pl.ds(pl.multiple_of(n * tile, tile), tile)

    def forward(n):
        cols = tiles(n)

        def step(i, carry):
            k, group = i // 2, lax.rem(i, 2)
            pre_gate = product(x_all, k, group, f_gate, cols)
            sigma = jax.nn.sigmoid(pre_gate)
            silu_val = pre_gate * sigma
            gated[k, group, :, cols] = silu_val
            slope[k, group, :, cols] = sigma * (1.0 + pre_gate * (1.0 - sigma))
            pre_up = product(x_all, k, group, f_up, cols)
            act[k, group, :, cols] = (gated[k, group, :, cols] * pre_up).astype(bf16)
            slope[k, group, :, cols] = slope[k, group, :, cols] * pre_up
            return carry

        lax.fori_loop(0, 4, step, 0)

    def backward(n):
        cols = tiles(n)

        def step(i, carry):
            k, group = i // 2, lax.rem(i, 2)
            back = product(dy_all, k, group, f_down, cols)
            d_gate[k, group, :, cols] = (back * slope[k, group, :, cols]).astype(bf16)
            d_up[k, group, :, cols] = (back * gated[k, group, :, cols]).astype(bf16)
            part = jnp.sum(act[k, group, :, cols].astype(f32) * back, axis=1, keepdims=True)
            whole = jnp.broadcast_to(part, gates_own.shape[2:])
            gates_own[k, group] = whole if n == 0 else gates_own[k, group] + whole
            return carry

        lax.fori_loop(0, 4, step, 0)

    def moved(m, i, n):
        return remote(strip(terms.at[m, i], 0, n), strip(arrived.at[m, i], 0, n), sum_send.at[m, i, n],
                      sum_recv.at[m, i, n], 2 * chip + core, beside)

    def gradients(i, n, sent):
        shard = jnp.where(i == 0, 3 - beside, jnp.where(i == 1, beside, jnp.where(i == 2, across, plane)))
        cols = pl.ds(pl.multiple_of(shard * depth, 128), depth)
        over = (((0,), (0,)), ((), ()))
        for m, left, right in ((0, x_all, d_gate), (1, x_all, d_up), (2, dy_all, act)):
            total = None
            for k in range(2):
                for group in range(2):
                    term = lax.dot_general(left[k, group, :, cols], right[k, group, :, tiles(n)], over,
                                           preferred_element_type=f32)
                    total = term if total is None else total + term
            terms[m, i, :, tiles(n)] = total.astype(bf16)
            if sent:
                moved(m, i, n).start()

    info_swap().wait()
    for copy in swaps(0):
        copy.wait_recv()
    dispatch(0, 1)
    spread(0, 1)
    pass_on(0, 0)
    for copy in swaps(1):
        copy.wait_recv()
    dispatch(1, 1)
    start_relay(0, 0)
    pass_on(0, 1)
    spread(1, 1)
    start_relay(1, 0)
    pass_on(1, 0)
    start_relay(2, 0)
    pass_on(1, 1)
    for n in range(parts):
        for m in range(2):
            weights_here(m, n)
        if n == 0:
            for group in range(2):
                landed(x_all.at[1 - core, group], hand_recv.at[0, group])
        forward(n)
        if n + 1 < parts:
            start_relay(0, n + 1)
        weights_here(2, n)
        if n == 0:
            for group in range(2):
                landed(dy_all.at[1 - core, group], hand_recv.at[1, group])
        backward(n)
        if n + 1 < parts:
            start_relay(1, n + 1)
            start_relay(2, n + 1)

        def first(i, carry, n=n):
            gradients(i, n, True)
            return carry

        lax.fori_loop(0, 2, first, 0)

    def rest(i, carry):
        gradients(2 + i // parts, lax.rem(i, parts), False)
        return carry

    lax.fori_loop(0, 2 * parts, rest, 0)

    for n in range(2):
        for group in range(2):
            hand_over(n, group).wait_send()

    def replies(k, group, other):
        wide = min(model_width, 512)

        def step(n, carry):
            cols = pl.ds(pl.multiple_of(n * wide, wide), wide)
            contract = (((1,), (1,)), ((), ()))
            total = lax.dot_general(d_gate[k, group], f_gate[cols], contract, preferred_element_type=f32)
            total = total + lax.dot_general(d_up[k, group], f_up[cols], contract, preferred_element_type=f32)
            if other is not None:
                total = total + other[group, :, cols].astype(f32)
            x_all[k, group, :, cols] = total.astype(bf16)
            return carry

        lax.fori_loop(0, model_width // wide, step, 0)

    gates_pass = remote(gates_own.at[1 - core], gates_in, pass_send.at[2], pass_recv.at[2], sibling, plane)
    gates_pass.start()

    def reply_pass(group):
        return remote(x_all.at[1 - core, group], reply_in.at[group], pass_send.at[group], pass_recv.at[group],
                      sibling, plane)

    for group in (1, 0):
        replies(1 - core, group, None)
        reply_pass(group).start()
    gates_pass.wait()
    gates_own[core] = gates_own[core] + gates_in[...]
    for group in (1, 0):
        reply_pass(group).wait()
        replies(core, group, reply_in)

        def send(k, carry, group=group):
            to = lax.rem(chip + k, chips)
            for n, (own, back) in enumerate(((x_all, reply_back), (gates_own, gates_back))):
                remote(block(own.at[core], group, to), block(back, group, chip), back_send.at[n, group],
                       back_recv.at[n, group], 2 * to + core, plane).start()
            return carry

        for n, (own, back) in enumerate(((x_all, reply_back), (gates_own, gates_back))):
            pltpu.make_async_copy(block(own.at[core], group, chip), block(back, group, chip),
                                  back_recv.at[n, group]).start()
        lax.fori_loop(1, chips, send, 0)

    def combine(group):
        landed(reply_back.at[group], back_recv.at[0, group])
        landed(gates_back.at[group], back_recv.at[1, group])
        chosen = picks(0, group)
        for j in range(chunks):
            cols = slice(j * half, (j + 1) * half)
            total = lax.dot_general(chosen, reply_back[group, :, cols], (((0,), (0,)), ((), ())),
                                    preferred_element_type=f32)
            dy_all[0, group, 0:tok_count, cols] = total.astype(bf16)
        gates_mix[group] = jnp.zeros(gates_mix.shape[1:], f32)
        for k, hit in enumerate(hits(group)):
            values = jnp.where(hit, gates_back[group, :, 0:1], 0.0)
            gates_mix[group, k:k + 1, 0:tok_count] = jnp.sum(values, axis=0, keepdims=True)

    def mixed(group):
        if group == 0:
            return []
        rows = dy_all.at[0, 1, pl.ds(0, tok_count)]
        return [remote(rows, mix_in, mix_send.at[1, 0], mix_recv.at[0], ep, across),
                remote(gates_mix.at[1], gates_mixed, mix_send.at[1, 1], mix_recv.at[1], ep, across)]

    for n in range(parts):
        if n == parts - 1:
            for group in (1, 0):
                combine(group)
                for copy in mixed(group):
                    copy.start()
        for i in range(2):
            if i == 1 and n == parts - 1:
                for copy in mixed(1):
                    copy.wait()
                mix_own = dy_all.at[0, 0]
                for j in range(chunks):
                    cols = slice(j * half, (j + 1) * half)
                    total = mix_own[0:tok_count, cols].astype(f32) + mix_in[:, cols].astype(f32)
                    mix_in[:, cols] = total.astype(bf16)
                for k in range(2):
                    gates_mix[0, k:k + 1, 0:tok_count] = gates_mix[0, k:k + 1, 0:tok_count] + gates_mixed[k:k + 1, 0:tok_count]
                finals = [pltpu.make_async_copy(mix_in, token_out, mix_send.at[0, 0]),
                          pltpu.make_async_copy(gates_mix.at[0], gates_out, mix_send.at[0, 1])]
                for copy in finals:
                    copy.start()
            for m in range(3):
                moved(m, i, n).wait()
                step = 128

                def add(k, carry, m=m, i=i, n=n):
                    rows = pl.ds(pl.multiple_of(k * step, step), step)
                    total = terms[m, 2 + i, rows, tiles(n)].astype(f32) + arrived[m, i, rows, tiles(n)].astype(f32)
                    terms[m, 2 + i, rows, tiles(n)] = total.astype(bf16)
                    return carry

                lax.fori_loop(0, depth // step, add, 0)
                done, out = strip(terms.at[m, 2 + i], 0, n), strip(grads[m], core, n)
                if i == 0:
                    remote(done, out, out_send.at[m, 0, n], out_recv.at[m, core, n],
                           2 * chip + parity, across).start()
                else:
                    @pl.when(core == parity)
                    def _(m=m, n=n, done=done, out=out):
                        pltpu.make_async_copy(done, out, out_recv.at[m, core, n]).start()

                    @pl.when(core != parity)
                    def _(m=m, n=n, done=done, out=out):
                        remote(done, out, out_send.at[m, 1, n], out_recv.at[m, core, n],
                               2 * chip + parity, plane).start()

    for n in range(parts):
        for m in range(3):
            landed(shard_strip(m, across, n), relay_send.at[m, n])
            for part in range(2):
                landed(strip(weights[m], part, n), weight_send.at[m, n, part])

            @pl.when(jnp.logical_not(away))
            def _(m=m, n=n):
                landed(strip(weights[m], 0, n), weight_send.at[m, n, 2])
            landed(strip(terms.at[m, 2], 0, n), out_send.at[m, 0, n])

            @pl.when(core != parity)
            def _(m=m, n=n):
                landed(strip(terms.at[m, 3], 0, n), out_send.at[m, 1, n])
            for part in range(2):
                landed(strip(grads[m], part, n), out_recv.at[m, part, n])
    for n in range(2):
        for copy in swaps(n):
            copy.wait_send()
    for n, own in enumerate((x_all, gates_own)):
        for group in range(2):
            landed(own.at[core, group, pl.ds(0, (chips - 1) * ROWS)], back_send.at[n, group])
    for copy in finals:
        copy.wait()


def shards(tokens, upstream, expert_ids, gate_values, w_gate, w_up, w_down):
    experts = lax.axis_size("ep")
    chips = experts // 2
    tok_count, top_count = expert_ids.shape
    model_width = tokens.shape[1]
    depth, width = w_gate.shape[1:]
    half = width // 2
    bf16 = jnp.bfloat16
    lanes = -(-tok_count // 128) * 128
    anywhere = pl.BlockSpec(memory_space=pl.ANY)
    dma = pltpu.SemaphoreType.DMA
    tall = chips * ROWS
    rows_buffer = pltpu.VMEM((2, 2, tall, model_width), bf16)
    full_buffer = pltpu.VMEM((4 * depth, half), bf16)
    wide_buffer = pltpu.VMEM((2, 2, tall, half), jnp.float32)
    narrow_buffer = pltpu.VMEM((2, 2, tall, half), bf16)
    grad_shape = jax.ShapeDtypeStruct((3, depth, width), bf16)
    mix_shape = jax.ShapeDtypeStruct((tok_count, model_width), bf16)
    info_shape = jax.ShapeDtypeStruct((8, lanes), jnp.float32)
    parts = max(1, half // 256)
    token_grad, gate_grad, grads = pl.pallas_call(
        functools.partial(layer_kernel, chips),
        out_shape=[mix_shape, info_shape, grad_shape],
        in_specs=[anywhere] * 2 + [pl.BlockSpec(memory_space=pltpu.VMEM)] * 2 + [anywhere] * 3,
        out_specs=[anywhere] * 3,
        scratch_shapes=[
            rows_buffer, rows_buffer, full_buffer, full_buffer, full_buffer,
            wide_buffer, wide_buffer, narrow_buffer, narrow_buffer, narrow_buffer,
            pltpu.VMEM((3, 4, depth, half), bf16), pltpu.VMEM((3, 2, depth, half), bf16),
            pltpu.VMEM((2, tall, model_width), bf16), pltpu.VMEM((2, tall, model_width), bf16),
            pltpu.VMEM((2, 2, tall, 128), jnp.float32), pltpu.VMEM((2, tall, 128), jnp.float32),
            pltpu.VMEM((2, tall, 128), jnp.float32), pltpu.VMEM((2, 8, lanes), jnp.float32),
            pltpu.VMEM((8, lanes), jnp.float32), pltpu.VMEM((8, lanes), jnp.float32), pltpu.VMEM((tok_count, model_width), bf16),
            pltpu.VMEM((8, lanes), jnp.float32),
            dma((2, model_width // half)), dma((2, model_width // half)), dma((2, model_width // half)),
            dma((2,)), dma((2, 2)),
            dma((2, 2)), dma((2, 2)), dma((2, 2)), dma((2, 2)),
            dma((3, parts, 3)), dma((3, parts, 3)), dma((3, parts, PIECES)), dma((3, parts)),
            dma((3, 2, parts)), dma((3, 2, parts)), dma((3,)), dma((3,)), dma((3, 2, parts)), dma((3, 2, parts)),
            dma((2, 2)), dma((2, 2)),
            dma((2, 2)), dma((2,))],
        compiler_params=pltpu.CompilerParams(has_side_effects=True, collective_id=0, vmem_limit_bytes=60 << 20),
        name="expert_layer",
    )(tokens, upstream, expert_ids.T, gate_values.T, w_gate[0], w_up[0], w_down[0])

    gate_grad = gate_grad[:top_count, :tok_count].T
    gate_grad = (gate_grad / gate_values.astype(jnp.float32)).astype(bf16)
    return token_grad, gate_grad, grads[0:1], grads[1:2], grads[2:3]


def solution(mesh):
    tokens_spec, weights_spec = P(("ep", "edp"), None), P("ep", "edp", None)
    return jax.shard_map(
        shards, mesh=mesh,
        in_specs=(tokens_spec,) * 4 + (weights_spec,) * 3,
        out_specs=(tokens_spec,) * 2 + (weights_spec,) * 3,
        check_vma=False,
    )
```
